32 devices in a mesh: row: 4 (over y, x), col: 8 (over z, core).
Axes of the slice: x: 2, y: 2, z: 4, core: 2. Of those that a mesh axis runs over, the one named last changes fastest.
Arguments:
- a_matrix: bfloat16 [4096, 4096], P('row', 'col'), may hold values from -0.09375 to 0.09375
- omega: bfloat16 [96, 4096], P(None, 'col'), may hold values from -6 to 6
- col_scale: float32 [4096], P('col'), may hold values from 1 to 48
- cone_point: float32 [4096], P('row'), may hold values from -8 to 8, as said below
- cone_id: int32 [4096], P('row'), may hold values from 0 to 4095, as said below
- cone_kind: int32 [4096], P('row'), may hold values from 0 to 1, as said below
Outputs:
- q_basis: float32 [96, 4096], P(None, 'col')
- r_factor: float32 [96, 96], replicated
The draws below stay inside these ranges and needn't reach their ends.
Inputs may be any that keep to these rules, and one draw needn't show every extreme that they name: `cone_id`: rows of one cone are consecutive and share one id, the index of the cone's first row; every cone lies inside an aligned block of 4 rows; the last row is a cone of its own. `cone_kind`: 1 marks a second-order cone, 0 nonnegative entries; equal on all rows of a cone; 1 only on cones of two rows or more. `cone_point`: on a second-order cone every non-head entry has magnitude 0.5 or more, and the head's magnitude is at most 0.95 times the norm of the other entries.
All inputs are finite; a program needn't handle non-finite values.
Results may differ from the reference program's by a relative error of at most 0.014.
Values may be sent and summed in bfloat16 or wider, within the bound.
No kernel may reach another device: no remote copies, remote signals or barrier semaphores. Data moves between devices by JAX's collectives and lax.ppermute only.
A program may use at most 64 MiB of HBM per device.

```python
import jax
import jax.numpy as jnp
from jax import lax

SKETCH = 96
COL_DEV = 512
R_DEV = 1024
CONE_SPAN = 4
PASSES = 2
VARS = 4096
ROWS = 4096
N_ROW = 4
N_COL = 8


def cone_layout(key):
    base = jax.random.fold_in(key, 7)
    first_key, second_key = jax.random.split(base)
    total = R_DEV * N_ROW
    positions = jnp.arange(total, dtype=jnp.int32)
    cuts = (jax.random.randint(first_key, (total,), 0, 3) == 0) | (positions % CONE_SPAN == 0) | (positions == total - 1)
    starts = lax.cummax(jnp.where(cuts, positions, 0), axis=0).astype(jnp.int32)
    cone_ids = starts
    sizes = jax.ops.segment_sum(jnp.ones((total,), jnp.int32), cone_ids, num_segments=total)[cone_ids]
    coin = jax.random.randint(second_key, (total,), 0, 2)
    kinds = jnp.where(sizes >= 2, coin[starts], 0).astype(jnp.int32)
    return (cone_ids, kinds, cuts)


def draw_cone_id(key, part):
    return cone_layout(key)[0]


def draw_cone_kind(key, part):
    return cone_layout(key)[1]


def draw_cone_point(key, part):
    cone_ids, kinds, cuts = cone_layout(key)
    total = R_DEV * N_ROW
    float_key = jax.random.fold_in(key, 11)
    mag_key, sign_key, head_key, drawn_key = jax.random.split(float_key, 4)
    signs = jnp.where(jax.random.randint(sign_key, (total,), 0, 2) == 0, -1.0, 1.0)
    magnitude = jax.random.uniform(mag_key, (total,), jnp.float32, 0.5, 2.0)
    share = jax.random.uniform(head_key, (total,), jnp.float32, -0.8, 0.8)
    drawn = jax.random.normal(drawn_key, (total,), jnp.float32)
    second_order = kinds == 1
    tail_vals = jnp.where(second_order & ~cuts, signs * magnitude, 0.0)
    tail_norm = jnp.sqrt(jax.ops.segment_sum(tail_vals * tail_vals, cone_ids, num_segments=total)[cone_ids])
    soc_vals = jnp.where(cuts, share * tail_norm, tail_vals)
    return jnp.where(second_order, soc_vals, drawn).astype(jnp.float32)


def draw_col_scale(key, part):
    total = COL_DEV * N_COL
    positions = jnp.arange(total).astype(jnp.float32)
    base = jnp.exp(jax.random.uniform(key, (total,), jnp.float32, 0.0, jnp.log(10.0)))
    return (base * (1.0 + 2.0 * positions / (total - 1))).astype(jnp.float32)


def steps_of(key, dims, cuts, low, high):
    level, own = 1.0, jax.random.fold_in(key, 6)
    for position, blocks in cuts:
        steps = jnp.exp(jax.random.uniform(jax.random.fold_in(own, position), (blocks,), jnp.float32, low / len(cuts), high / len(cuts)))
        level = level * jnp.repeat(steps, dims[position] // blocks).reshape([-1 if axis == position else 1 for axis in range(len(dims))])
    return level


def centred(own_key, dims, scale, bound, pieces=(), held_as=jnp.bfloat16):
    factor_of = steps_of(own_key, dims, pieces, -0.22, 0.18) if pieces else 1.0
    array = jax.random.normal(own_key, dims, jnp.float32) * scale * factor_of
    return jnp.minimum(jnp.maximum(array, -bound), bound).astype(held_as)


def setup_inputs(seed: int = 0) -> dict:
    key_of = jax.random.split(jax.random.key(seed), 7)
    a_matrix = centred(key_of[0], (ROWS, VARS), VARS ** -0.5, 0.09375, ((0, 4), (1, 8)))
    omega = centred(key_of[1], (SKETCH, VARS), 1.0, 6.0, ((1, 8),))
    col_scale = draw_col_scale(jax.random.fold_in(key_of[6], 71), 0)
    cone_point = draw_cone_point(jax.random.fold_in(key_of[6], 71), 0)
    cone_id = draw_cone_id(jax.random.fold_in(key_of[6], 71), 0)
    cone_kind = draw_cone_kind(jax.random.fold_in(key_of[6], 71), 0)
    return {"a_matrix": a_matrix, "omega": omega, "col_scale": col_scale, "cone_point": cone_point, "cone_id": cone_id, "cone_kind": cone_kind}


def apply_cones(sketch_rows, cone_point, cone_id, cone_kind):
    total = cone_point.shape[0]
    values = sketch_rows.T
    previous = jnp.concatenate([cone_id[:1] - 1, cone_id[:-1]])
    is_head = cone_id != previous
    second_order = cone_kind == 1

    def segment(vals):
        return jax.ops.segment_sum(vals, cone_id, num_segments=total)[cone_id]
    tail_vals = jnp.where(second_order & ~is_head, cone_point, jnp.float32(0.0))
    tail_norm = jnp.sqrt(jnp.where(second_order, segment(tail_vals * tail_vals), jnp.float32(1.0)))
    head_val = segment(jnp.where(is_head, cone_point, jnp.float32(0.0)))
    cone_ratio = (head_val / tail_norm)[:, None]
    unit_tail = (tail_vals / tail_norm)[:, None]
    head_part = segment(jnp.where(is_head[:, None], values, jnp.float32(0.0)))
    projected = segment(unit_tail * values)
    soc_out = jnp.where(is_head[:, None], 0.5 * (head_part + projected), 0.5 * (unit_tail * head_part + (1.0 + cone_ratio) * values - cone_ratio * unit_tail * projected))
    positive = jnp.where(cone_point > 0, jnp.float32(1.0), jnp.float32(0.0))[:, None]
    result = jnp.where(second_order[:, None], soc_out, positive * values)
    return result.T

def reference(a_matrix, omega, col_scale, cone_point, cone_id, cone_kind):
    vectors = omega
    for repeat in range(PASSES):
        scaled = (vectors.astype(jnp.float32) * col_scale[None, :]).astype(jnp.bfloat16)
        sketch_rows = lax.dot_general(scaled.astype(jnp.float32), a_matrix.astype(jnp.float32), (((1,), (1,)), ((), ())), preferred_element_type=jnp.float32)
        weighted = apply_cones(sketch_rows, cone_point, cone_id, cone_kind).astype(jnp.bfloat16)
        back = jnp.dot(weighted.astype(jnp.float32), a_matrix.astype(jnp.float32), preferred_element_type=jnp.float32) * col_scale[None, :]
        gram_matrix = jnp.dot(back, back.T, precision=lax.Precision.HIGHEST) / VARS
        lower_factor = jnp.linalg.cholesky(gram_matrix)
        orth_basis = lax.linalg.triangular_solve(lower_factor, back, left_side=True, lower=True)
        vectors = orth_basis.astype(jnp.bfloat16)
    return (orth_basis, lower_factor.T)
```

```python
import functools

import jax
import jax.numpy as jnp
from jax import lax
from jax.experimental import pallas as pl
from jax.experimental.pallas import tpu as pltpu
from jax.sharding import PartitionSpec as P

LANES = 128
HIGHEST = lax.Precision.HIGHEST
F32 = jnp.float32
BF16 = jnp.bfloat16
NT = (((1,), (1,)), ((), ()))

VMEM = pl.BlockSpec(memory_space=pltpu.VMEM)
SMEM = pl.BlockSpec(memory_space=pltpu.SMEM)


def call(body, outs, args, scratch=(), scalars=0):
    return pl.pallas_call(
        body,
        out_shape=outs,
        in_specs=[SMEM] * scalars + [VMEM] * (len(args) - scalars),
        out_specs=jax.tree.map(lambda _: VMEM, outs),
        scratch_shapes=list(scratch),
        compiler_params=pltpu.CompilerParams(vmem_limit_bytes=16 * 1024 * 1024),
    )(*args)


def partner(value, axis, mask):
    size = lax.axis_size(axis)
    return lax.ppermute(value, axis, [(i, i ^ mask) for i in range(size)])


def tree_sum(terms):
    while len(terms) > 1:
        terms = [terms[i] + terms[i + 1] for i in range(0, len(terms), 2)]
    return terms[0]


def split_blocks(total, first, send_ref, keep_ref, pieces):
    half = pieces // 2
    for place in range(half):
        for ref, odd in ((keep_ref, 0), (send_ref, 1)):
            block = jnp.bitwise_xor(first, 2 * place + odd)
            start = pl.multiple_of(block * LANES, LANES)
            ref[:, place * LANES : (place + 1) * LANES] = total[:, pl.ds(start, LANES)].astype(ref.dtype)


def first_rows_kernel(pieces, first_ref, omega_ref, scale_ref, a_ref, send_ref, keep_ref, total):
    scaled = (omega_ref[...].astype(F32) * scale_ref[...]).astype(BF16)
    total[...] = lax.dot_general(scaled, a_ref[...], NT, preferred_element_type=F32)
    split_blocks(total, first_ref[0], send_ref, keep_ref, pieces)


def next_rows_kernel(pieces, terms, first_ref, *refs):
    parts, (scale_ref, a_ref, send_ref, keep_ref, back_ref, total) = refs[:terms], refs[terms:]
    scale = scale_ref[...]
    back = tree_sum([part[...].astype(F32) for part in parts]) * scale
    back_ref[...] = back
    scaled = (back * scale).astype(BF16)
    total[...] = lax.dot_general(scaled, a_ref[...], NT, preferred_element_type=F32)
    split_blocks(total, first_ref[0], send_ref, keep_ref, pieces)


def pair_kernel(places, keep_ref, got_ref, own_ref, *send_refs):
    for place in range(places):
        cols = slice(place * LANES, (place + 1) * LANES)
        value = keep_ref[:, cols] + got_ref[:, cols].astype(F32)
        if place == 0:
            own_ref[...] = value
        else:
            send_refs[place - 1][...] = value.astype(BF16)


def cone_kernel(point_ref, point_col_ref, id_ref, id_col_ref, kind_ref, kind_col_ref, base_ref, out_ref):
    length = out_ref.shape[0]
    base = base_ref[0]
    point, point_col = point_ref[...], point_col_ref[...]
    ids, ids_col = id_ref[...], id_col_ref[...]
    soc, soc_col = kind_ref[...] == 1, kind_col_ref[...] == 1
    head = ids == base + lax.broadcasted_iota(jnp.int32, (1, length), 1)
    head_col = ids_col == base + lax.broadcasted_iota(jnp.int32, (length, 1), 0)
    same = (ids_col == ids).astype(F32)
    eye = (
        lax.broadcasted_iota(jnp.int32, (length, length), 0)
        == lax.broadcasted_iota(jnp.int32, (length, length), 1)
    ).astype(F32)
    tail = jnp.where(soc & ~head, point, 0.0)
    tail_col = jnp.where(soc_col & ~head_col, point_col, 0.0)
    norm = jnp.sqrt(jnp.where(soc, jnp.sum(same * (tail_col * tail_col), axis=0, keepdims=True), 1.0))
    norm_col = jnp.sqrt(jnp.where(soc_col, jnp.sum(same * (tail * tail), axis=1, keepdims=True), 1.0))
    head_val = jnp.sum(same * jnp.where(head_col, point_col, 0.0), axis=0, keepdims=True)
    ratio = head_val / norm
    unit, unit_col = tail / norm, tail_col / norm_col
    head_out = 0.5 * (eye + unit_col)
    tail_out = 0.5 * (
        unit * jnp.where(head_col, 1.0, 0.0) + (1.0 + ratio) * eye - ratio * unit * unit_col
    )
    soc_f, head_f = soc.astype(F32), head.astype(F32)
    soc_out = head_f * head_out + (1.0 - head_f) * tail_out
    plain = eye * jnp.where(point > 0, 1.0, 0.0)
    out_ref[...] = same * (soc_f * soc_out + (1.0 - soc_f) * plain)


def weigh_kernel(own_ref, *refs):
    parts, (cone_ref, out_ref) = refs[:-2], refs[-2:]
    total = tree_sum([own_ref[...]] + [part[...].astype(F32) for part in parts])
    out_ref[...] = jnp.dot(total, cone_ref[...], precision=HIGHEST, preferred_element_type=F32).astype(BF16)


def back_kernel(order, first_ref, *refs):
    pieces = len(order)
    parts, (a_ref, out_ref, rows) = refs[:pieces], refs[pieces:]
    for part, mask in zip(parts, order):
        start = pl.multiple_of(jnp.bitwise_xor(first_ref[0], mask) * LANES, LANES)
        rows[:, pl.ds(start, LANES)] = part[...]
    out_ref[...] = jnp.dot(rows[...], a_ref[...], preferred_element_type=F32).astype(BF16)


def gram_kernel(terms, *refs):
    parts, (back_one_ref, scale_ref, gram_ref, back_ref) = refs[:terms], refs[terms:]
    width = back_one_ref.shape[0]
    back = tree_sum([part[...].astype(F32) for part in parts]) * scale_ref[...]
    back_ref[...] = back
    unit = 1.0 / jnp.maximum(jnp.max(jnp.abs(back), keepdims=True), 1e-37)
    back = back * unit
    one = back_one_ref[...]
    gram_ref[0] = jnp.zeros(gram_ref.shape[1:], F32) + unit
    gram_ref[1] = jnp.zeros(gram_ref.shape[1:], F32)
    gram_ref[0, :, :width] = lax.dot_general(back, back, NT, precision=HIGHEST, preferred_element_type=F32)
    gram_ref[1, :, :width] = lax.dot_general(one, one, NT, precision=HIGHEST, preferred_element_type=F32)


def merge_grams(grams, width):
    units = [gram[0][:1, width : width + 1] for gram in grams]
    unit = functools.reduce(jnp.minimum, units)
    second = tree_sum([gram[0][:, :width] * ((unit / own) * (unit / own)) for gram, own in zip(grams, units)])
    first = tree_sum([gram[1][:, :width] for gram in grams])
    return second, first, unit


def merge_kernel(*refs):
    grams, out_ref = refs[:-1], refs[-1]
    width = out_ref.shape[1]
    second, first, unit = merge_grams(grams, width)
    out_ref[0] = jnp.zeros(out_ref.shape[1:], F32) + unit
    out_ref[1] = jnp.zeros(out_ref.shape[1:], F32)
    out_ref[0, :, :width] = second
    out_ref[1, :, :width] = first


def levels_of(size):
    levels, shift = [], 0
    while size > 1:
        radix = 2 if shift == 0 or size == 2 else 4
        levels.append([k << shift for k in range(1, radix)])
        shift += radix // 2
        size //= radix
    return levels


def local(a_matrix, omega, col_scale, cone_point, cone_id, cone_kind):
    width = omega.shape[0]
    rows, cols = a_matrix.shape
    n_col = lax.axis_size("col")
    n_row = lax.axis_size("row")
    pieces = rows // LANES
    total_cols = cols * n_col
    here = lax.axis_index("col")
    block = lax.rem(here, pieces)
    first = block.reshape(1)
    scale = col_scale.reshape(1, cols)

    places = pieces // 2
    z_masks = [2 * place for place in range(1, places)]
    levels = levels_of(n_col)
    outer = [[mask for mask in masks if mask >= pieces] for masks in levels]
    outer = [masks for masks in outer if masks]

    with jax.named_scope("cone"):
        start = block * LANES
        vectors = [lax.dynamic_slice_in_dim(v, start, LANES) for v in (cone_point, cone_id, cone_kind)]
        base = (lax.axis_index("row") * rows + start).reshape(1)
        cone_args = [v.reshape(shape) for v in vectors for shape in ((1, LANES), (LANES, 1))]
        cone = pl.pallas_call(
            cone_kernel,
            out_shape=jax.ShapeDtypeStruct((LANES, LANES), F32),
            in_specs=[VMEM] * 6 + [SMEM],
            out_specs=VMEM,
        )(*cone_args, base)

    send_shape = jax.ShapeDtypeStruct((width, rows // 2), BF16)
    keep_shape = jax.ShapeDtypeStruct((width, rows // 2), F32)
    back_shape = jax.ShapeDtypeStruct((width, cols), F32)
    part_shape = jax.ShapeDtypeStruct((width, cols), BF16)
    piece_f32 = jax.ShapeDtypeStruct((width, LANES), F32)
    piece_bf16 = jax.ShapeDtypeStruct((width, LANES), BF16)
    total = pltpu.VMEM((width, rows), F32)

    def exchange(send, keep):
        got = partner(send, "col", 1)
        own, *sends = call(
            functools.partial(pair_kernel, places), [piece_f32] + [piece_bf16] * (places - 1), (keep, got)
        )
        parts = [partner(value, "col", mask) for value, mask in zip(sends, z_masks)]
        for masks in outer:
            own = tree_sum([own] + [part.astype(F32) for part in parts])
            parts = [partner(own, "col", mask) for mask in masks]
        weighted = call(weigh_kernel, piece_bf16, (own, *parts, cone))
        held = [weighted] + [partner(weighted, "col", mask) for mask in z_masks]
        across = [partner(value, "col", 1) for value in held]
        order = [0] + z_masks
        order = order + [mask ^ 1 for mask in order]
        part = call(
            functools.partial(back_kernel, order),
            part_shape,
            (first, *held, *across, a_matrix),
            scratch=(pltpu.VMEM((width, rows), BF16),),
            scalars=1,
        )
        return [part] + [partner(part, "row", mask) for mask in range(1, n_row)]

    with jax.named_scope("pass_one"):
        send, keep = call(
            functools.partial(first_rows_kernel, pieces),
            [send_shape, keep_shape],
            (first, omega, scale, a_matrix),
            scratch=(total,),
            scalars=1,
        )
        parts = exchange(send, keep)
    with jax.named_scope("pass_two"):
        send, keep, back_one = call(
            functools.partial(next_rows_kernel, pieces, n_row),
            [send_shape, keep_shape, back_shape],
            (first, *parts, scale, a_matrix),
            scratch=(total,),
            scalars=1,
        )
        parts = exchange(send, keep)

    with jax.named_scope("gram"):
        gram_shape = jax.ShapeDtypeStruct((2, width, LANES), F32)
        gram, back = call(
            functools.partial(gram_kernel, n_row), [gram_shape, back_shape], (*parts, back_one, scale)
        )
        for masks in levels[:-1]:
            grams = [gram] + [partner(gram, "col", mask) for mask in masks]
            second, first_gram, unit = merge_grams(grams, width)
            gram = jnp.concatenate(
                [
                    jnp.stack([second, first_gram]),
                    jnp.broadcast_to(unit, (2, width, LANES - width)),
                ],
                axis=2,
            )
        grams = [gram] + [partner(gram, "col", mask) for mask in levels[-1]]
        second, first_gram, unit = merge_grams(grams, width)
        lower = jnp.linalg.cholesky(jnp.stack([second, first_gram]) / total_cols)
        basis = lax.linalg.triangular_solve(lower[0], back * unit, left_side=True, lower=True)
        factor = lax.linalg.triangular_solve(lower[1], lower[0], left_side=True, lower=True) / unit
    return basis, factor.T


def solution(mesh):
    in_specs = (P("row", "col"), P(None, "col"), P("col"), P("row"), P("row"), P("row"))
    out_specs = (P(None, "col"), P())
    return jax.shard_map(local, mesh=mesh, in_specs=in_specs, out_specs=out_specs, check_vma=False)
```

```python
import functools

import jax
import jax.numpy as jnp
from jax import lax
from jax.experimental import pallas as pl
from jax.experimental.pallas import tpu as pltpu
from jax.sharding import PartitionSpec as P

LANES = 128
HIGHEST = lax.Precision.HIGHEST
F32 = jnp.float32
BF16 = jnp.bfloat16
NT = (((1,), (1,)), ((), ()))
CONE_SPAN = 4
SHIFTS = tuple(range(1 - CONE_SPAN, CONE_SPAN))

VMEM = pl.BlockSpec(memory_space=pltpu.VMEM)
SMEM = pl.BlockSpec(memory_space=pltpu.SMEM)


def call(body, outs, args, scratch=(), scalars=0):
    return pl.pallas_call(
        body,
        out_shape=outs,
        in_specs=[SMEM] * scalars + [VMEM] * (len(args) - scalars),
        out_specs=jax.tree.map(lambda _: VMEM, outs),
        scratch_shapes=list(scratch),
        compiler_params=pltpu.CompilerParams(vmem_limit_bytes=16 * 1024 * 1024),
    )(*args)


def partner(value, axis, mask):
    size = lax.axis_size(axis)
    return lax.ppermute(value, axis, [(i, i ^ mask) for i in range(size)])


def tree_sum(terms):
    while len(terms) > 1:
        terms = [terms[i] + terms[i + 1] for i in range(0, len(terms), 2)]
    return terms[0]


def halves(a_ref, core_ref):
    half = a_ref.shape[0] // 2
    starts = (core_ref[0] * half, (1 - core_ref[0]) * half)
    return [a_ref[pl.ds(pl.multiple_of(start, half), half), :] for start in starts]


def project(scaled, a_ref, core_ref, keep_ref, send_ref):
    kept, sent = halves(a_ref, core_ref)
    send_ref[...] = lax.dot_general(scaled, sent, NT, preferred_element_type=F32).astype(BF16)
    keep_ref[...] = lax.dot_general(scaled, kept, NT, preferred_element_type=F32)


def first_rows_kernel(core_ref, omega_ref, scale_ref, a_ref, keep_ref, send_ref):
    scaled = (omega_ref[...].astype(F32) * scale_ref[...]).astype(BF16)
    project(scaled, a_ref, core_ref, keep_ref, send_ref)


def next_rows_kernel(terms, core_ref, *refs):
    parts, (scale_ref, a_ref, keep_ref, send_ref, back_ref) = refs[:terms], refs[terms:]
    scale = scale_ref[...]
    back = tree_sum([part[...].astype(F32) for part in parts]) * scale
    back_ref[...] = back
    project((back * scale).astype(BF16), a_ref, core_ref, keep_ref, send_ref)


def add_kernel(own_ref, *refs):
    parts, (keep_ref, send_ref) = refs[:-2], refs[-2:]
    total = tree_sum([own_ref[...]] + [part[...].astype(F32) for part in parts])
    keep_ref[...] = total
    send_ref[...] = total.astype(BF16)


def shifted(value, shift):
    if shift == 0:
        return value
    return pltpu.roll(value, (-shift) % value.shape[-1], value.ndim - 1)


def cone_kernel(base_ref, point_ref, id_ref, kind_ref, out_ref):
    shape = point_ref.shape
    point, ids = point_ref[...], id_ref[...]
    soc = kind_ref[...] == 1
    place = lax.broadcasted_iota(jnp.int32, shape, 0) * LANES + lax.broadcasted_iota(jnp.int32, shape, 1)
    head = jnp.where(ids == base_ref[0] + place, 1.0, 0.0)
    same = {s: jnp.where(shifted(ids, s) == ids, 1.0, 0.0) for s in SHIFTS}
    tail = jnp.where(soc, point * (1.0 - head), 0.0)
    square = sum(same[s] * shifted(tail * tail, s) for s in SHIFTS)
    norm = jnp.sqrt(jnp.where(soc, square, 1.0))
    ratio = sum(same[s] * shifted(head * point, s) for s in SHIFTS) / norm
    unit = tail / norm
    plain = jnp.where(point > 0, 1.0, 0.0)
    for number, s in enumerate(SHIFTS):
        eye = 1.0 if s == 0 else 0.0
        other = shifted(unit, s)
        at_head = 0.5 * (eye + other)
        at_tail = 0.5 * (unit * shifted(head, s) + (1.0 + ratio) * eye - ratio * unit * other)
        cone = head * at_head + (1.0 - head) * at_tail
        out_ref[number] = same[s] * jnp.where(soc, cone, plain * eye)


def weigh_kernel(core_ref, own_ref, *refs):
    parts, (cone_ref, out_ref) = refs[:-2], refs[-2:]
    blocks = out_ref.shape[1] // LANES
    for block in range(blocks):
        cols = slice(block * LANES, (block + 1) * LANES)
        total = tree_sum([own_ref[:, cols]] + [part[:, cols].astype(F32) for part in parts])
        row = core_ref[0] * blocks + block
        terms = [cone_ref[number, pl.ds(row, 1), :] * shifted(total, s) for number, s in enumerate(SHIFTS)]
        out_ref[:, cols] = sum(terms).astype(BF16)


def back_kernel(core_ref, held_ref, got_ref, a_ref, out_ref):
    kept, sent = halves(a_ref, core_ref)
    total = jnp.dot(held_ref[...], kept, preferred_element_type=F32)
    total += jnp.dot(got_ref[...], sent, preferred_element_type=F32)
    out_ref[...] = total.astype(BF16)


def gram_kernel(terms, *refs):
    parts, (back_one_ref, scale_ref, gram_ref, back_ref) = refs[:terms], refs[terms:]
    width = back_one_ref.shape[0]
    back = tree_sum([part[...].astype(F32) for part in parts]) * scale_ref[...]
    back_ref[...] = back
    unit = 1.0 / jnp.maximum(jnp.max(jnp.abs(back), keepdims=True), 1e-37)
    back = back * unit
    one = back_one_ref[...]
    gram_ref[0] = jnp.zeros(gram_ref.shape[1:], F32) + unit
    gram_ref[1] = jnp.zeros(gram_ref.shape[1:], F32)
    gram_ref[0, :, :width] = lax.dot_general(back, back, NT, precision=HIGHEST, preferred_element_type=F32)
    gram_ref[1, :, :width] = lax.dot_general(one, one, NT, precision=HIGHEST, preferred_element_type=F32)


def merge_grams(grams, width):
    units = [gram[0][:1, width : width + 1] for gram in grams]
    unit = functools.reduce(jnp.minimum, units)
    second = tree_sum([gram[0][:, :width] * ((unit / own) * (unit / own)) for gram, own in zip(grams, units)])
    first = tree_sum([gram[1][:, :width] for gram in grams])
    return second, first, unit


def merge_kernel(*refs):
    *grams, out_ref = refs
    width = out_ref.shape[1]
    second, first, unit = merge_grams(grams, width)
    out_ref[0] = jnp.zeros(out_ref.shape[1:], F32) + unit
    out_ref[1] = jnp.zeros(out_ref.shape[1:], F32)
    out_ref[0, :, :width] = second
    out_ref[1, :, :width] = first


def levels_of(size):
    levels, shift = [], 0
    while size > 1:
        radix = 2 if shift == 0 or size == 2 else 4
        levels.append([k << shift for k in range(1, radix)])
        shift += radix // 2
        size //= radix
    return levels


def local(a_matrix, omega, col_scale, cone_point, cone_id, cone_kind):
    width = omega.shape[0]
    rows, cols = a_matrix.shape
    n_col = lax.axis_size("col")
    n_row = lax.axis_size("row")
    here = lax.axis_index("col")
    total_cols = cols * n_col
    core = lax.rem(here, 2).reshape(1)
    scale = col_scale.reshape(1, cols)
    core_masks, *chip_levels = levels_of(n_col)

    def shape(*dims, dtype=F32):
        return jax.ShapeDtypeStruct(dims, dtype)

    half_f32, half_bf16 = shape(width, rows // 2), shape(width, rows // 2, dtype=BF16)
    back_f32, back_bf16 = shape(width, cols), shape(width, cols, dtype=BF16)

    with jax.named_scope("cone"):
        base = (lax.axis_index("row") * rows).reshape(1)
        vectors = [v.reshape(rows // LANES, LANES) for v in (cone_point, cone_id, cone_kind)]
        cone = call(cone_kernel, shape(len(SHIFTS), rows // LANES, LANES), (base, *vectors), scalars=1)

    def exchange(keep, send):
        parts = [partner(send, "col", mask) for mask in core_masks]
        for masks in chip_levels:
            keep, send = call(add_kernel, [half_f32, half_bf16], (keep, *parts))
            parts = [partner(send, "col", mask) for mask in masks]
        weighted = call(weigh_kernel, half_bf16, (core, keep, *parts, cone), scalars=1)
        got = partner(weighted, "col", core_masks[0])
        part = call(back_kernel, back_bf16, (core, weighted, got, a_matrix), scalars=1)
        return [part] + [partner(part, "row", mask) for mask in range(1, n_row)]

    with jax.named_scope("pass_one"):
        keep, send = call(first_rows_kernel, [half_f32, half_bf16], (core, omega, scale, a_matrix), scalars=1)
        parts = exchange(keep, send)
    with jax.named_scope("pass_two"):
        keep, send, back_one = call(
            functools.partial(next_rows_kernel, n_row),
            [half_f32, half_bf16, back_f32],
            (core, *parts, scale, a_matrix),
            scalars=1,
        )
        parts = exchange(keep, send)

    with jax.named_scope("gram"):
        gram_shape = shape(2, width, LANES)
        gram, back = call(functools.partial(gram_kernel, n_row), [gram_shape, back_f32], (*parts, back_one, scale))
        levels = [core_masks] + chip_levels
        for masks in levels[:-1]:
            gram = call(merge_kernel, gram_shape, [gram] + [partner(gram, "col", mask) for mask in masks])
        grams = [gram] + [partner(gram, "col", mask) for mask in levels[-1]]
        second, first_gram, unit = merge_grams(grams, width)
        lower = jnp.linalg.cholesky(jnp.stack([second, first_gram]) / total_cols)
        basis = lax.linalg.triangular_solve(lower[0], back * unit, left_side=True, lower=True)
        factor = lax.linalg.triangular_solve(lower[1], lower[0], left_side=True, lower=True) / unit
    return basis, factor.T


def solution(mesh):
    in_specs = (P("row", "col"), P(None, "col"), P("col"), P("row"), P("row"), P("row"))
    out_specs = (P(None, "col"), P())
    return jax.shard_map(local, mesh=mesh, in_specs=in_specs, out_specs=out_specs, check_vma=False)
```

```python
import functools

import jax
import jax.numpy as jnp
from jax import lax
from jax.experimental import pallas as pl
from jax.experimental.pallas import tpu as pltpu
from jax.sharding import PartitionSpec as P

LANES = 128
SUBLANES = 8
HIGHEST = lax.Precision.HIGHEST
F32 = jnp.float32
BF16 = jnp.bfloat16
NT = (((1,), (1,)), ((), ()))
CONE_SPAN = 4
SHIFTS = tuple(range(1 - CONE_SPAN, CONE_SPAN))

VMEM = pl.BlockSpec(memory_space=pltpu.VMEM)
SMEM = pl.BlockSpec(memory_space=pltpu.SMEM)


def call(body, outs, args, scratch=(), scalars=0):
    return pl.pallas_call(
        body,
        out_shape=outs,
        in_specs=[SMEM] * scalars + [VMEM] * (len(args) - scalars),
        out_specs=jax.tree.map(lambda _: VMEM, outs),
        scratch_shapes=list(scratch),
        compiler_params=pltpu.CompilerParams(vmem_limit_bytes=16 * 1024 * 1024),
    )(*args)


def partner(value, axis, mask):
    size = lax.axis_size(axis)
    return lax.ppermute(value, axis, [(i, i ^ mask) for i in range(size)])


def tree_sum(terms):
    while len(terms) > 1:
        terms = [terms[i] + terms[i + 1] for i in range(0, len(terms), 2)]
    return terms[0]


def halves(a_ref, core_ref):
    half = a_ref.shape[0] // 2
    starts = (core_ref[0] * half, (1 - core_ref[0]) * half)
    return [a_ref[pl.ds(pl.multiple_of(start, half), half), :] for start in starts]


def project(scaled, a_ref, core_ref, keep_ref, send_ref):
    kept, sent = halves(a_ref, core_ref)
    send_ref[...] = lax.dot_general(scaled, sent, NT, preferred_element_type=F32).astype(BF16)
    keep_ref[...] = lax.dot_general(scaled, kept, NT, preferred_element_type=F32)


def first_rows_kernel(core_ref, omega_ref, scale_ref, a_ref, keep_ref, send_ref):
    scaled = (omega_ref[...].astype(F32) * scale_ref[...]).astype(BF16)
    project(scaled, a_ref, core_ref, keep_ref, send_ref)


def next_rows_kernel(terms, core_ref, *refs):
    parts, (scale_ref, a_ref, keep_ref, send_ref, back_ref) = refs[:terms], refs[terms:]
    scale = scale_ref[...]
    back = tree_sum([part[...].astype(F32) for part in parts]) * scale
    back_ref[...] = back
    project((back * scale).astype(BF16), a_ref, core_ref, keep_ref, send_ref)


def add_kernel(own_ref, *refs):
    parts, (keep_ref, send_ref) = refs[:-2], refs[-2:]
    total = tree_sum([own_ref[...]] + [part[...].astype(F32) for part in parts])
    keep_ref[...] = total
    send_ref[...] = total.astype(BF16)


def shifted(value, shift):
    if shift == 0:
        return value
    return pltpu.roll(value, (-shift) % value.shape[-1], value.ndim - 1)


def cone_kernel(base_ref, point_ref, id_ref, kind_ref, out_ref):
    shape = point_ref.shape
    point, ids = point_ref[...], id_ref[...]
    soc = kind_ref[...] == 1
    place = lax.broadcasted_iota(jnp.int32, shape, 0) * LANES + lax.broadcasted_iota(jnp.int32, shape, 1)
    head = jnp.where(ids == base_ref[0] + place, 1.0, 0.0)
    same = {s: jnp.where(shifted(ids, s) == ids, 1.0, 0.0) for s in SHIFTS}
    tail = jnp.where(soc, point * (1.0 - head), 0.0)
    square = sum(same[s] * shifted(tail * tail, s) for s in SHIFTS)
    norm = jnp.sqrt(jnp.where(soc, square, 1.0))
    ratio = sum(same[s] * shifted(head * point, s) for s in SHIFTS) / norm
    unit = tail / norm
    plain = jnp.where(point > 0, 1.0, 0.0)
    for number, s in enumerate(SHIFTS):
        eye = 1.0 if s == 0 else 0.0
        other = shifted(unit, s)
        at_head = 0.5 * (eye + other)
        at_tail = 0.5 * (unit * shifted(head, s) + (1.0 + ratio) * eye - ratio * unit * other)
        cone = head * at_head + (1.0 - head) * at_tail
        out_ref[number] = same[s] * jnp.where(soc, cone, plain * eye)


def weigh_kernel(core_ref, own_ref, *refs):
    parts, (cone_ref, out_ref) = refs[:-2], refs[-2:]
    blocks = out_ref.shape[1] // LANES
    for block in range(blocks):
        cols = slice(block * LANES, (block + 1) * LANES)
        total = tree_sum([own_ref[:, cols]] + [part[:, cols].astype(F32) for part in parts])
        row = core_ref[0] * blocks + block
        terms = [cone_ref[number, pl.ds(row, 1), :] * shifted(total, s) for number, s in enumerate(SHIFTS)]
        out_ref[:, cols] = sum(terms).astype(BF16)


def back_kernel(core_ref, held_ref, got_ref, a_ref, out_ref):
    kept, sent = halves(a_ref, core_ref)
    total = jnp.dot(held_ref[...], kept, preferred_element_type=F32)
    total += jnp.dot(got_ref[...], sent, preferred_element_type=F32)
    out_ref[...] = total.astype(BF16)


def gram_kernel(terms, *refs):
    parts, (back_one_ref, scale_ref, gram_ref, back_ref) = refs[:terms], refs[terms:]
    width = back_one_ref.shape[0]
    back = tree_sum([part[...].astype(F32) for part in parts]) * scale_ref[...]
    back_ref[...] = back
    unit = 1.0 / jnp.maximum(jnp.max(jnp.abs(back), keepdims=True), 1e-37)
    back = back * unit
    one = back_one_ref[...]
    gram_ref[0] = jnp.zeros(gram_ref.shape[1:], F32) + unit
    gram_ref[1] = jnp.zeros(gram_ref.shape[1:], F32)
    gram_ref[0, :, :width] = lax.dot_general(back, back, NT, precision=HIGHEST, preferred_element_type=F32)
    gram_ref[1, :, :width] = lax.dot_general(one, one, NT, precision=HIGHEST, preferred_element_type=F32)


def merge_grams(grams, width):
    units = [gram[0][:1, width : width + 1] for gram in grams]
    unit = functools.reduce(jnp.minimum, units)
    second = tree_sum([gram[0][:, :width] * ((unit / own) * (unit / own)) for gram, own in zip(grams, units)])
    first = tree_sum([gram[1][:, :width] for gram in grams])
    return second, first, unit


def merge_kernel(*refs):
    *grams, out_ref = refs
    width = out_ref.shape[1]
    second, first, unit = merge_grams(grams, width)
    out_ref[0] = jnp.zeros(out_ref.shape[1:], F32) + unit
    out_ref[1] = jnp.zeros(out_ref.shape[1:], F32)
    out_ref[0, :, :width] = second
    out_ref[1, :, :width] = first


def splat(value, width):
    return jnp.broadcast_to(value, (SUBLANES, width))


def eliminate_tile(upper, inverse, tile):
    size = upper[0].shape[1]
    first = tile * SUBLANES
    below = range(tile + 1, len(upper))
    steps = range(SUBLANES)
    rows = [splat(upper[tile][t : t + 1, :], size) for t in steps]
    others = [splat(inverse[tile][t : t + 1, :], size) for t in steps]
    corner = {(t, u): splat(rows[t][:, first + u : first + u + 1], size) for t in steps for u in range(t, SUBLANES)}
    columns = [{i: splat(upper[i][:, first + t : first + t + 1], size) for i in below} for t in steps]
    inverted = []
    for t in steps:
        inverted.append(1.0 / corner[t, t])
        for u in range(t + 1, SUBLANES):
            factor = corner[t, u] * inverted[t]
            for w in range(u, SUBLANES):
                corner[u, w] = corner[u, w] - factor * corner[t, w]
            rows[u] = rows[u] - factor * rows[t]
            others[u] = others[u] - factor * others[t]
            for i in below:
                columns[u][i] = columns[u][i] - factor * columns[t][i]
    for i in below:
        factors = [columns[t][i] * inverted[t] for t in steps]
        upper[i] = upper[i] - sum(f * row for f, row in zip(factors, rows))
        inverse[i] = inverse[i] - sum(f * row for f, row in zip(factors, others))
    sub = lax.broadcasted_iota(jnp.int32, (SUBLANES, size), 0)
    pivots, upper[tile], inverse[tile] = corner[0, 0], rows[0], others[0]
    for t in steps[1:]:
        pivots = jnp.where(sub == t, corner[t, t], pivots)
        upper[tile] = jnp.where(sub == t, rows[t], upper[tile])
        inverse[tile] = jnp.where(sub == t, others[t], inverse[tile])
    root = 1.0 / jnp.sqrt(pivots)
    upper[tile], inverse[tile] = upper[tile] * root, inverse[tile] * root


def eliminate(grams):
    size = grams[0].shape[0]
    tiles = range(size // SUBLANES)
    sub = lax.broadcasted_iota(jnp.int32, (SUBLANES, size), 0)
    lane = lax.broadcasted_iota(jnp.int32, (SUBLANES, size), 1)
    uppers = [[gram[i * SUBLANES : (i + 1) * SUBLANES, :] for i in tiles] for gram in grams]
    inverses = [[jnp.where(sub + i * SUBLANES == lane, 1.0, 0.0) for i in tiles] for _ in grams]
    for tile in tiles:
        for upper, inverse in zip(uppers, inverses):
            eliminate_tile(upper, inverse, tile)
    return [(jnp.concatenate(upper, axis=0), jnp.concatenate(inverse, axis=0)) for upper, inverse in zip(uppers, inverses)]


def factor_kernel(total_cols, *refs):
    *grams, back_ref, basis_ref, factor_ref = refs
    width = back_ref.shape[0]
    second, first, unit = merge_grams(grams, width)
    (upper, inverse), (_, inverse_one) = eliminate([gram * (1.0 / total_cols) for gram in (second, first)])
    basis_ref[...] = jnp.dot(inverse, back_ref[...] * unit, precision=HIGHEST, preferred_element_type=F32)
    row = lax.broadcasted_iota(jnp.int32, (width, width), 0)
    col = lax.broadcasted_iota(jnp.int32, (width, width), 1)
    upper = jnp.where(row <= col, upper, 0.0)
    factor = lax.dot_general(upper, inverse_one, NT, precision=HIGHEST, preferred_element_type=F32)
    factor_ref[...] = factor / unit


def levels_of(size):
    levels, mask = [[1]], 2
    while mask < size:
        levels.append([mask])
        if 2 * mask < size:
            levels.append([3 * mask])
        mask *= 4
    return levels


def local(a_matrix, omega, col_scale, cone_point, cone_id, cone_kind):
    width = omega.shape[0]
    rows, cols = a_matrix.shape
    n_col = lax.axis_size("col")
    n_row = lax.axis_size("row")
    here = lax.axis_index("col")
    total_cols = cols * n_col
    core = lax.rem(here, 2).reshape(1)
    scale = col_scale.reshape(1, cols)
    core_masks, *chip_levels = levels_of(n_col)

    def shape(*dims, dtype=F32):
        return jax.ShapeDtypeStruct(dims, dtype)

    half_f32, half_bf16 = shape(width, rows // 2), shape(width, rows // 2, dtype=BF16)
    back_f32, back_bf16 = shape(width, cols), shape(width, cols, dtype=BF16)

    with jax.named_scope("cone"):
        base = (lax.axis_index("row") * rows).reshape(1)
        vectors = [v.reshape(rows // LANES, LANES) for v in (cone_point, cone_id, cone_kind)]
        cone = call(cone_kernel, shape(len(SHIFTS), rows // LANES, LANES), (base, *vectors), scalars=1)

    def exchange(keep, send):
        parts = [partner(send, "col", mask) for mask in core_masks]
        for masks in chip_levels:
            keep, send = call(add_kernel, [half_f32, half_bf16], (keep, *parts))
            parts = [partner(send, "col", mask) for mask in masks]
        weighted = call(weigh_kernel, half_bf16, (core, keep, *parts, cone), scalars=1)
        got = partner(weighted, "col", core_masks[0])
        part = call(back_kernel, back_bf16, (core, weighted, got, a_matrix), scalars=1)
        return [part] + [partner(part, "row", mask) for mask in range(1, n_row)]

    with jax.named_scope("pass_one"):
        keep, send = call(first_rows_kernel, [half_f32, half_bf16], (core, omega, scale, a_matrix), scalars=1)
        parts = exchange(keep, send)
    with jax.named_scope("pass_two"):
        keep, send, back_one = call(
            functools.partial(next_rows_kernel, n_row),
            [half_f32, half_bf16, back_f32],
            (core, *parts, scale, a_matrix),
            scalars=1,
        )
        parts = exchange(keep, send)

    with jax.named_scope("gram"):
        gram_shape = shape(2, width, LANES)
        gram, back = call(functools.partial(gram_kernel, n_row), [gram_shape, back_f32], (*parts, back_one, scale))
        levels = [core_masks] + chip_levels
        for masks in levels[:-1]:
            gram = call(merge_kernel, gram_shape, [gram] + [partner(gram, "col", mask) for mask in masks])
        grams = [gram] + [partner(gram, "col", mask) for mask in levels[-1]]
        basis, factor = call(
            functools.partial(factor_kernel, total_cols), [back_f32, shape(width, width)], (*grams, back)
        )
    return basis, factor


def solution(mesh):
    in_specs = (P("row", "col"), P(None, "col"), P("col"), P("row"), P("row"), P("row"))
    out_specs = (P(None, "col"), P())
    return jax.shard_map(local, mesh=mesh, in_specs=in_specs, out_specs=out_specs, check_vma=False)
```

```python
import functools

import jax
import jax.numpy as jnp
from jax import lax
from jax.experimental import pallas as pl
from jax.experimental.pallas import tpu as pltpu
from jax.sharding import PartitionSpec as P

LANES = 128
SUBLANES = 8
HIGHEST = lax.Precision.HIGHEST
F32 = jnp.float32
BF16 = jnp.bfloat16
NT = (((1,), (1,)), ((), ()))
CONE_SPAN = 4
SHIFTS = tuple(range(1 - CONE_SPAN, CONE_SPAN))

VMEM_LIMIT = 16 * 1024 * 1024
VMEM = pl.BlockSpec(memory_space=pltpu.VMEM)
SMEM = pl.BlockSpec(memory_space=pltpu.SMEM)


def call(body, outs, args, scalars=0, flops=0):
    return pl.pallas_call(
        body,
        out_shape=outs,
        in_specs=[SMEM] * scalars + [VMEM] * (len(args) - scalars),
        out_specs=jax.tree.map(lambda _: VMEM, outs),
        cost_estimate=pl.CostEstimate(flops=flops, bytes_accessed=flops // 96, transcendentals=0) if flops else None,
        compiler_params=pltpu.CompilerParams(vmem_limit_bytes=VMEM_LIMIT),
    )(*args)


def partner(value, axis, mask):
    size = lax.axis_size(axis)
    return lax.ppermute(value, axis, [(i, i ^ mask) for i in range(size)])


def tree_sum(terms):
    while len(terms) > 1:
        terms = [terms[i] + terms[i + 1] for i in range(0, len(terms), 2)]
    return terms[0]


def half_start(rows, core, kept):
    half = rows // 2
    return pl.multiple_of((core if kept else 1 - core) * half, half)


def half_rows(a_ref, core_ref, kept):
    rows = a_ref.shape[0]
    return a_ref[pl.ds(half_start(rows, core_ref[0], kept), rows // 2), :]


def project(scaled, a_half):
    return lax.dot_general(scaled, a_half, NT, preferred_element_type=F32)


def first_send_kernel(core_ref, scaled_ref, a_ref, send_ref):
    send_ref[...] = project(scaled_ref[...], half_rows(a_ref, core_ref, False)).astype(BF16)


def next_send_kernel(terms, core_ref, *refs):
    parts, (scale_ref, a_ref, send_ref, scaled_ref, back_ref) = refs[:terms], refs[terms:]
    scale = scale_ref[...]
    back = tree_sum([part[...].astype(F32) for part in parts]) * scale
    back_ref[...] = back
    scaled = (back * scale).astype(BF16)
    scaled_ref[...] = scaled
    send_ref[...] = project(scaled, half_rows(a_ref, core_ref, False)).astype(BF16)


def keep_kernel(core_ref, scaled_ref, a_ref, keep_ref):
    keep_ref[...] = project(scaled_ref[...], half_rows(a_ref, core_ref, True))


def add_kernel(own_ref, *refs):
    parts, (keep_ref, send_ref) = refs[:-2], refs[-2:]
    total = tree_sum([own_ref[...]] + [part[...].astype(F32) for part in parts])
    keep_ref[...] = total
    send_ref[...] = total.astype(BF16)


def shifted(value, shift):
    if shift == 0:
        return value
    return pltpu.roll(value, (-shift) % value.shape[-1], value.ndim - 1)


def cone_kernel(base_ref, point_ref, id_ref, kind_ref, out_ref):
    shape = point_ref.shape
    point, ids = point_ref[...], id_ref[...]
    soc = kind_ref[...] == 1
    place = lax.broadcasted_iota(jnp.int32, shape, 0) * LANES + lax.broadcasted_iota(jnp.int32, shape, 1)
    head = jnp.where(ids == base_ref[0] + place, 1.0, 0.0)
    same = {s: jnp.where(shifted(ids, s) == ids, 1.0, 0.0) for s in SHIFTS}
    tail = jnp.where(soc, point * (1.0 - head), 0.0)
    square = sum(same[s] * shifted(tail * tail, s) for s in SHIFTS)
    norm = jnp.sqrt(jnp.where(soc, square, 1.0))
    ratio = sum(same[s] * shifted(head * point, s) for s in SHIFTS) / norm
    unit = tail / norm
    plain = jnp.where(point > 0, 1.0, 0.0)
    for number, s in enumerate(SHIFTS):
        eye = 1.0 if s == 0 else 0.0
        other = shifted(unit, s)
        at_head = 0.5 * (eye + other)
        at_tail = 0.5 * (unit * shifted(head, s) + (1.0 + ratio) * eye - ratio * unit * other)
        cone = head * at_head + (1.0 - head) * at_tail
        out_ref[number] = same[s] * jnp.where(soc, cone, plain * eye)


def weigh_kernel(core_ref, own_ref, *refs):
    parts, (cone_ref, out_ref) = refs[:-2], refs[-2:]
    blocks = out_ref.shape[1] // LANES
    for block in range(blocks):
        cols = slice(block * LANES, (block + 1) * LANES)
        total = tree_sum([own_ref[:, cols]] + [part[:, cols].astype(F32) for part in parts])
        row = core_ref[0] * blocks + block
        terms = [cone_ref[number, pl.ds(row, 1), :] * shifted(total, s) for number, s in enumerate(SHIFTS)]
        out_ref[:, cols] = sum(terms).astype(BF16)


def back_kept_kernel(core_ref, held_ref, a_ref, out_ref):
    out_ref[...] = jnp.dot(held_ref[...], half_rows(a_ref, core_ref, True), preferred_element_type=F32)


def back_kernel(core_ref, kept_ref, got_ref, a_ref, out_ref):
    sent = jnp.dot(got_ref[...], half_rows(a_ref, core_ref, False), preferred_element_type=F32)
    out_ref[...] = (kept_ref[...] + sent).astype(BF16)


def packed_places(width):
    row = lax.broadcasted_iota(jnp.int32, (width, LANES), 0)
    lane = lax.broadcasted_iota(jnp.int32, (width, LANES), 1)
    return lane <= row, lane <= width


def gram_kernel(terms, *refs):
    parts, (back_one_ref, scale_ref, gram_ref, back_ref) = refs[:terms], refs[terms:]
    width, cols = back_ref.shape
    back = tree_sum([part[...].astype(F32) for part in parts]) * scale_ref[...]
    back_ref[...] = back
    unit = 1.0 / jnp.maximum(jnp.max(jnp.abs(back), keepdims=True), 1e-37)
    blank = jnp.zeros((LANES - width, cols), F32)

    def gram(value):
        padded = jnp.concatenate([value, blank], axis=0)
        return lax.dot_general(value, padded, NT, precision=HIGHEST, preferred_element_type=F32)

    in_second, in_first = packed_places(width)
    first = pltpu.roll(gram(back_one_ref[...]), 1, 1)
    gram_ref[...] = jnp.where(in_second, gram(back * unit), jnp.where(in_first, first, unit))


def merge_grams(grams):
    width = grams[0].shape[0]
    units = [gram[:1, LANES - 1 :] for gram in grams]
    unit = functools.reduce(jnp.minimum, units)
    in_second, in_first = packed_places(width)
    grams = [gram[...] for gram in grams]
    second = tree_sum([gram * ((unit / own) * (unit / own)) for gram, own in zip(grams, units)])
    return jnp.where(in_second, second, jnp.where(in_first, tree_sum(grams), unit)), unit


def merge_kernel(*refs):
    *grams, out_ref = refs
    out_ref[...] = merge_grams(grams)[0]


def unpack_grams(packed):
    width = packed.shape[0]
    row = lax.broadcasted_iota(jnp.int32, (width, width), 0)
    lane = lax.broadcasted_iota(jnp.int32, (width, width), 1)
    lower = packed[:, :width]
    upper = pltpu.roll(packed, LANES - 1, 1)[:, :width]
    return jnp.where(lane <= row, lower, lower.T), jnp.where(lane >= row, upper, upper.T)


def splat(value, width):
    return jnp.broadcast_to(value, (SUBLANES, width))


def eliminate_tile(upper, inverse, tile):
    size = upper[0].shape[1]
    first = tile * SUBLANES
    below = range(tile + 1, len(upper))
    steps = range(SUBLANES)
    rows = [splat(upper[tile][t : t + 1, :], size) for t in steps]
    others = [splat(inverse[tile][t : t + 1, :], size) for t in steps]
    corner = {(t, u): splat(rows[t][:, first + u : first + u + 1], size) for t in steps for u in range(t, SUBLANES)}
    columns = [{i: splat(upper[i][:, first + t : first + t + 1], size) for i in below} for t in steps]
    inverted = []
    for t in steps:
        inverted.append(1.0 / corner[t, t])
        for u in range(t + 1, SUBLANES):
            factor = corner[t, u] * inverted[t]
            for w in range(u, SUBLANES):
                corner[u, w] = corner[u, w] - factor * corner[t, w]
            rows[u] = rows[u] - factor * rows[t]
            others[u] = others[u] - factor * others[t]
            for i in below:
                columns[u][i] = columns[u][i] - factor * columns[t][i]
    for i in below:
        factors = [columns[t][i] * inverted[t] for t in steps]
        upper[i] = upper[i] - sum(f * row for f, row in zip(factors, rows))
        inverse[i] = inverse[i] - sum(f * row for f, row in zip(factors, others))
    sub = lax.broadcasted_iota(jnp.int32, (SUBLANES, size), 0)
    pivots, upper[tile], inverse[tile] = corner[0, 0], rows[0], others[0]
    for t in steps[1:]:
        pivots = jnp.where(sub == t, corner[t, t], pivots)
        upper[tile] = jnp.where(sub == t, rows[t], upper[tile])
        inverse[tile] = jnp.where(sub == t, others[t], inverse[tile])
    root = 1.0 / jnp.sqrt(pivots)
    upper[tile], inverse[tile] = upper[tile] * root, inverse[tile] * root


def eliminate(grams):
    size = grams[0].shape[0]
    tiles = range(size // SUBLANES)
    sub = lax.broadcasted_iota(jnp.int32, (SUBLANES, size), 0)
    lane = lax.broadcasted_iota(jnp.int32, (SUBLANES, size), 1)
    uppers = [[gram[i * SUBLANES : (i + 1) * SUBLANES, :] for i in tiles] for gram in grams]
    inverses = [[jnp.where(sub + i * SUBLANES == lane, 1.0, 0.0) for i in tiles] for _ in grams]
    for tile in tiles:
        for upper, inverse in zip(uppers, inverses):
            eliminate_tile(upper, inverse, tile)
    return [(jnp.concatenate(upper, axis=0), jnp.concatenate(inverse, axis=0)) for upper, inverse in zip(uppers, inverses)]


def factor_kernel(total_cols, *refs):
    *grams, back_ref, basis_ref, factor_ref = refs
    width = back_ref.shape[0]
    packed, unit = merge_grams(grams)
    (upper, inverse), (_, inverse_one) = eliminate([gram * (1.0 / total_cols) for gram in unpack_grams(packed)])
    basis_ref[...] = jnp.dot(inverse, back_ref[...] * unit, precision=HIGHEST, preferred_element_type=F32)
    row = lax.broadcasted_iota(jnp.int32, (width, width), 0)
    col = lax.broadcasted_iota(jnp.int32, (width, width), 1)
    upper = jnp.where(row <= col, upper, 0.0)
    factor = lax.dot_general(upper, inverse_one, NT, precision=HIGHEST, preferred_element_type=F32)
    factor_ref[...] = factor / unit


def levels_of(size):
    levels, mask = [[1]], 2
    while mask < size:
        levels.append([mask])
        if 2 * mask < size:
            levels.append([3 * mask])
        mask *= 4
    return levels


def local(a_matrix, omega, col_scale, cone_point, cone_id, cone_kind):
    width = omega.shape[0]
    rows, cols = a_matrix.shape
    n_col = lax.axis_size("col")
    n_row = lax.axis_size("row")
    here = lax.axis_index("col")
    total_cols = cols * n_col
    core = lax.rem(here, 2).reshape(1)
    scale = col_scale.reshape(1, cols)
    core_masks, *chip_levels = levels_of(n_col)

    def shape(*dims, dtype=F32):
        return jax.ShapeDtypeStruct(dims, dtype)

    half_f32, half_bf16 = shape(width, rows // 2), shape(width, rows // 2, dtype=BF16)
    back_f32, back_bf16 = shape(width, cols), shape(width, cols, dtype=BF16)

    with jax.named_scope("cone"):
        base = (lax.axis_index("row") * rows).reshape(1)
        vectors = [v.reshape(rows // LANES, LANES) for v in (cone_point, cone_id, cone_kind)]
        cone = call(cone_kernel, shape(len(SHIFTS), rows // LANES, LANES), (base, *vectors), scalars=1)

    flops = width * rows * cols

    def exchange(keep, send):
        parts = [partner(send, "col", mask) for mask in core_masks]
        for masks in chip_levels:
            keep, send = call(add_kernel, [half_f32, half_bf16], (keep, *parts))
            parts = [partner(send, "col", mask) for mask in masks]
        weighted = call(weigh_kernel, half_bf16, (core, keep, *parts, cone), scalars=1)
        kept = call(back_kept_kernel, back_f32, (core, weighted, a_matrix), scalars=1, flops=flops)
        got = partner(weighted, "col", core_masks[0])
        part = call(back_kernel, back_bf16, (core, kept, got, a_matrix), scalars=1, flops=flops)
        return [part] + [partner(part, "row", mask) for mask in range(1, n_row)]

    with jax.named_scope("pass_one"):
        scaled = (omega.astype(F32) * scale).astype(BF16)
        send = call(first_send_kernel, half_bf16, (core, scaled, a_matrix), scalars=1)
        keep = call(keep_kernel, half_f32, (core, scaled, a_matrix), scalars=1, flops=flops)
        parts = exchange(keep, send)
    with jax.named_scope("pass_two"):
        send, scaled, back_one = call(
            functools.partial(next_send_kernel, n_row),
            [half_bf16, back_bf16, back_f32],
            (core, *parts, scale, a_matrix),
            scalars=1,
        )
        keep = call(keep_kernel, half_f32, (core, scaled, a_matrix), scalars=1, flops=flops)
        parts = exchange(keep, send)

    with jax.named_scope("gram"):
        gram_shape = shape(width, LANES)
        gram, back = call(functools.partial(gram_kernel, n_row), [gram_shape, back_f32], (*parts, back_one, scale))
        levels = [core_masks] + chip_levels
        for masks in levels[:-1]:
            gram = call(merge_kernel, gram_shape, [gram] + [partner(gram, "col", mask) for mask in masks])
        grams = [gram] + [partner(gram, "col", mask) for mask in levels[-1]]
        basis, factor = call(
            functools.partial(factor_kernel, total_cols), [back_f32, shape(width, width)], (*grams, back)
        )
    return basis, factor


def solution(mesh):
    in_specs = (P("row", "col"), P(None, "col"), P("col"), P("row"), P("row"), P("row"))
    out_specs = (P(None, "col"), P())
    return jax.shard_map(local, mesh=mesh, in_specs=in_specs, out_specs=out_specs, check_vma=False)
```

```python
import functools

import jax
import jax.numpy as jnp
from jax import lax
from jax.experimental import pallas as pl
from jax.experimental.pallas import tpu as pltpu
from jax.sharding import PartitionSpec as P

LANES = 128
SUBLANES = 8
HIGHEST = lax.Precision.HIGHEST
F32 = jnp.float32
BF16 = jnp.bfloat16
NT = (((1,), (1,)), ((), ()))
CONE_SPAN = 4
SHIFTS = tuple(range(1 - CONE_SPAN, CONE_SPAN))

VMEM_LIMIT = 16 * 1024 * 1024
VMEM = pl.BlockSpec(memory_space=pltpu.VMEM)
SMEM = pl.BlockSpec(memory_space=pltpu.SMEM)


def call(body, outs, args, scalars=0, flops=0):
    return pl.pallas_call(
        body,
        out_shape=outs,
        in_specs=[SMEM] * scalars + [VMEM] * (len(args) - scalars),
        out_specs=jax.tree.map(lambda _: VMEM, outs),
        cost_estimate=pl.CostEstimate(flops=flops, bytes_accessed=flops // 96, transcendentals=0) if flops else None,
        compiler_params=pltpu.CompilerParams(vmem_limit_bytes=VMEM_LIMIT),
    )(*args)


def partner(value, axis, mask, odd_mask=None):
    odd_mask = mask if odd_mask is None else odd_mask
    size = lax.axis_size(axis)
    return lax.ppermute(value, axis, [(i, i ^ (odd_mask if i % 2 else mask)) for i in range(size)])


def tree_sum(terms):
    while len(terms) > 1:
        terms = [terms[i] + terms[i + 1] for i in range(0, len(terms), 2)]
    return terms[0]


def half_start(rows, core, kept):
    half = rows // 2
    return pl.multiple_of((core if kept else 1 - core) * half, half)


def half_rows(a_ref, core_ref, kept):
    rows = a_ref.shape[0]
    return a_ref[pl.ds(half_start(rows, core_ref[0], kept), rows // 2), :]


def project(scaled, a_half):
    return lax.dot_general(scaled, a_half, NT, preferred_element_type=F32)


def first_send_kernel(core_ref, scaled_ref, a_ref, send_ref):
    send_ref[...] = project(scaled_ref[...], half_rows(a_ref, core_ref, False)).astype(BF16)


def next_send_kernel(terms, core_ref, *refs):
    parts, (scale_ref, a_ref, send_ref, scaled_ref, back_ref) = refs[:terms], refs[terms:]
    scale = scale_ref[...]
    back = tree_sum([part[...].astype(F32) for part in parts]) * scale
    back_ref[...] = back
    scaled = (back * scale).astype(BF16)
    scaled_ref[...] = scaled
    send_ref[...] = project(scaled, half_rows(a_ref, core_ref, False)).astype(BF16)


def keep_kernel(core_ref, scaled_ref, a_ref, keep_ref):
    keep_ref[...] = project(scaled_ref[...], half_rows(a_ref, core_ref, True))


def add_kernel(own_ref, *refs):
    parts, (keep_ref, send_ref) = refs[:-2], refs[-2:]
    total = tree_sum([own_ref[...]] + [part[...].astype(F32) for part in parts])
    keep_ref[...] = total
    send_ref[...] = total.astype(BF16)


def shifted(value, shift):
    if shift == 0:
        return value
    return pltpu.roll(value, (-shift) % value.shape[-1], value.ndim - 1)


def cone_kernel(base_ref, point_ref, id_ref, kind_ref, out_ref):
    shape = point_ref.shape
    point, ids = point_ref[...], id_ref[...]
    soc = kind_ref[...] == 1
    place = lax.broadcasted_iota(jnp.int32, shape, 0) * LANES + lax.broadcasted_iota(jnp.int32, shape, 1)
    head = jnp.where(ids == base_ref[0] + place, 1.0, 0.0)
    same = {s: jnp.where(shifted(ids, s) == ids, 1.0, 0.0) for s in SHIFTS}
    tail = jnp.where(soc, point * (1.0 - head), 0.0)
    square = sum(same[s] * shifted(tail * tail, s) for s in SHIFTS)
    norm = jnp.sqrt(jnp.where(soc, square, 1.0))
    ratio = sum(same[s] * shifted(head * point, s) for s in SHIFTS) / norm
    unit = tail / norm
    plain = jnp.where(point > 0, 1.0, 0.0)
    for number, s in enumerate(SHIFTS):
        eye = 1.0 if s == 0 else 0.0
        other = shifted(unit, s)
        at_head = 0.5 * (eye + other)
        at_tail = 0.5 * (unit * shifted(head, s) + (1.0 + ratio) * eye - ratio * unit * other)
        cone = head * at_head + (1.0 - head) * at_tail
        out_ref[number] = same[s] * jnp.where(soc, cone, plain * eye)


def weigh_kernel(core_ref, own_ref, *refs):
    parts, (cone_ref, out_ref) = refs[:-2], refs[-2:]
    blocks = out_ref.shape[1] // LANES
    for block in range(blocks):
        cols = slice(block * LANES, (block + 1) * LANES)
        total = tree_sum([own_ref[:, cols]] + [part[:, cols].astype(F32) for part in parts])
        row = core_ref[0] * blocks + block
        terms = [cone_ref[number, pl.ds(row, 1), :] * shifted(total, s) for number, s in enumerate(SHIFTS)]
        out_ref[:, cols] = sum(terms).astype(BF16)


def back_kept_kernel(core_ref, held_ref, a_ref, out_ref):
    out_ref[...] = jnp.dot(held_ref[...], half_rows(a_ref, core_ref, True), preferred_element_type=F32)


def back_kernel(core_ref, kept_ref, got_ref, a_ref, out_ref):
    sent = jnp.dot(got_ref[...], half_rows(a_ref, core_ref, False), preferred_element_type=F32)
    out_ref[...] = (kept_ref[...] + sent).astype(BF16)


def packed_places(width):
    row = lax.broadcasted_iota(jnp.int32, (width, LANES), 0)
    lane = lax.broadcasted_iota(jnp.int32, (width, LANES), 1)
    return lane <= row, lane <= width


def gram_of(value):
    width, cols = value.shape
    padded = jnp.concatenate([value, jnp.zeros((LANES - width, cols), F32)], axis=0)
    return lax.dot_general(value, padded, NT, precision=HIGHEST, preferred_element_type=F32)


def first_gram_kernel(back_ref, gram_ref):
    gram_ref[...] = pltpu.roll(gram_of(back_ref[...]), 1, 1)


def gram_kernel(terms, *refs):
    parts, (first_ref, scale_ref, gram_ref, back_ref) = refs[:terms], refs[terms:]
    back = tree_sum([part[...].astype(F32) for part in parts]) * scale_ref[...]
    back_ref[...] = back
    unit = 1.0 / jnp.maximum(jnp.max(jnp.abs(back), keepdims=True), 1e-37)
    in_second, in_first = packed_places(back.shape[0])
    gram_ref[...] = jnp.where(in_second, gram_of(back * unit), jnp.where(in_first, first_ref[...], unit))


def merge_grams(grams):
    width = grams[0].shape[0]
    units = [gram[:1, LANES - 1 :] for gram in grams]
    unit = functools.reduce(jnp.minimum, units)
    in_second, in_first = packed_places(width)
    grams = [gram[...] for gram in grams]
    second = tree_sum([gram * ((unit / own) * (unit / own)) for gram, own in zip(grams, units)])
    return jnp.where(in_second, second, jnp.where(in_first, tree_sum(grams), unit)), unit


def merge_kernel(*refs):
    *grams, out_ref = refs
    out_ref[...] = merge_grams(grams)[0]


def unpack_grams(packed):
    width = packed.shape[0]
    row = lax.broadcasted_iota(jnp.int32, (width, width), 0)
    lane = lax.broadcasted_iota(jnp.int32, (width, width), 1)
    lower = packed[:, :width]
    upper = pltpu.roll(packed, LANES - 1, 1)[:, :width]
    return jnp.where(lane <= row, lower, lower.T), jnp.where(lane >= row, upper, upper.T)


def splat(value, width):
    return jnp.broadcast_to(value, (SUBLANES, width))


def eliminate_tile(upper, inverse, tile):
    size = upper[0].shape[1]
    first = tile * SUBLANES
    below = range(tile + 1, len(upper))
    steps = range(SUBLANES)
    rows = [splat(upper[tile][t : t + 1, :], size) for t in steps]
    others = [splat(inverse[tile][t : t + 1, :], size) for t in steps]
    corner = {(t, u): splat(rows[t][:, first + u : first + u + 1], size) for t in steps for u in range(t, SUBLANES)}
    columns = [{i: splat(upper[i][:, first + t : first + t + 1], size) for i in below} for t in steps]
    inverted = []
    for t in steps:
        inverted.append(1.0 / corner[t, t])
        for u in range(t + 1, SUBLANES):
            factor = corner[t, u] * inverted[t]
            for w in range(u, SUBLANES):
                corner[u, w] = corner[u, w] - factor * corner[t, w]
            rows[u] = rows[u] - factor * rows[t]
            others[u] = others[u] - factor * others[t]
            for i in below:
                columns[u][i] = columns[u][i] - factor * columns[t][i]
    for i in below:
        factors = [columns[t][i] * inverted[t] for t in steps]
        upper[i] = upper[i] - sum(f * row for f, row in zip(factors, rows))
        inverse[i] = inverse[i] - sum(f * row for f, row in zip(factors, others))
    sub = lax.broadcasted_iota(jnp.int32, (SUBLANES, size), 0)
    pivots, upper[tile], inverse[tile] = corner[0, 0], rows[0], others[0]
    for t in steps[1:]:
        pivots = jnp.where(sub == t, corner[t, t], pivots)
        upper[tile] = jnp.where(sub == t, rows[t], upper[tile])
        inverse[tile] = jnp.where(sub == t, others[t], inverse[tile])
    root = 1.0 / jnp.sqrt(pivots)
    upper[tile], inverse[tile] = upper[tile] * root, inverse[tile] * root


def eliminate(grams):
    size = grams[0].shape[0]
    tiles = range(size // SUBLANES)
    sub = lax.broadcasted_iota(jnp.int32, (SUBLANES, size), 0)
    lane = lax.broadcasted_iota(jnp.int32, (SUBLANES, size), 1)
    uppers = [[gram[i * SUBLANES : (i + 1) * SUBLANES, :] for i in tiles] for gram in grams]
    inverses = [[jnp.where(sub + i * SUBLANES == lane, 1.0, 0.0) for i in tiles] for _ in grams]
    for tile in tiles:
        for upper, inverse in zip(uppers, inverses):
            eliminate_tile(upper, inverse, tile)
    return [(jnp.concatenate(upper, axis=0), jnp.concatenate(inverse, axis=0)) for upper, inverse in zip(uppers, inverses)]


def factor_kernel(total_cols, *refs):
    *grams, back_ref, basis_ref, factor_ref = refs
    width = back_ref.shape[0]
    packed, unit = merge_grams(grams)
    (upper, inverse), (_, inverse_one) = eliminate([gram * (1.0 / total_cols) for gram in unpack_grams(packed)])
    basis_ref[...] = jnp.dot(inverse, back_ref[...] * unit, precision=HIGHEST, preferred_element_type=F32)
    row = lax.broadcasted_iota(jnp.int32, (width, width), 0)
    col = lax.broadcasted_iota(jnp.int32, (width, width), 1)
    upper = jnp.where(row <= col, upper, 0.0)
    factor = lax.dot_general(upper, inverse_one, NT, precision=HIGHEST, preferred_element_type=F32)
    factor_ref[...] = factor / unit


def chip_rounds(size):
    rounds, mask = [], 2
    while mask < size:
        if 2 * mask < size:
            rounds += [(2 * mask, mask), (mask, 2 * mask)]
        else:
            rounds.append((mask, mask))
        mask *= 4
    return rounds


def direct_rounds(size):
    rounds, mask = [[1]], 2
    while mask < size:
        rounds.append([mask, 2 * mask, 3 * mask] if 2 * mask < size else [mask])
        mask *= 4
    return rounds


def local(a_matrix, omega, col_scale, cone_point, cone_id, cone_kind):
    width = omega.shape[0]
    rows, cols = a_matrix.shape
    n_col = lax.axis_size("col")
    n_row = lax.axis_size("row")
    here = lax.axis_index("col")
    total_cols = cols * n_col
    core = lax.rem(here, 2).reshape(1)
    scale = col_scale.reshape(1, cols)
    rounds = chip_rounds(n_col)

    def shape(*dims, dtype=F32):
        return jax.ShapeDtypeStruct(dims, dtype)

    half_f32, half_bf16 = shape(width, rows // 2), shape(width, rows // 2, dtype=BF16)
    back_f32, back_bf16 = shape(width, cols), shape(width, cols, dtype=BF16)

    with jax.named_scope("cone"):
        base = (lax.axis_index("row") * rows).reshape(1)
        vectors = [v.reshape(rows // LANES, LANES) for v in (cone_point, cone_id, cone_kind)]
        cone = call(cone_kernel, shape(len(SHIFTS), rows // LANES, LANES), (base, *vectors), scalars=1)

    flops = width * rows * cols

    def exchange(keep, send):
        got = partner(send, "col", 1)
        for masks in rounds:
            keep, send = call(add_kernel, [half_f32, half_bf16], (keep, got))
            got = partner(send, "col", *masks)
        weighted = call(weigh_kernel, half_bf16, (core, keep, got, cone), scalars=1)
        kept = call(back_kept_kernel, back_f32, (core, weighted, a_matrix), scalars=1, flops=flops)
        got = partner(weighted, "col", 1)
        part = call(back_kernel, back_bf16, (core, kept, got, a_matrix), scalars=1, flops=flops)
        return [part] + [partner(part, "row", mask) for mask in range(1, n_row)]

    with jax.named_scope("pass_one"):
        scaled = (omega.astype(F32) * scale).astype(BF16)
        send = call(first_send_kernel, half_bf16, (core, scaled, a_matrix), scalars=1)
        keep = call(keep_kernel, half_f32, (core, scaled, a_matrix), scalars=1, flops=flops)
        parts = exchange(keep, send)
    with jax.named_scope("pass_two"):
        send, scaled, back_one = call(
            functools.partial(next_send_kernel, n_row),
            [half_bf16, back_bf16, back_f32],
            (core, *parts, scale, a_matrix),
            scalars=1,
        )
        keep = call(keep_kernel, half_f32, (core, scaled, a_matrix), scalars=1, flops=flops)
        gram_shape = shape(width, LANES)
        first = call(first_gram_kernel, gram_shape, (back_one,), flops=flops // 4)
        parts = exchange(keep, send)

    with jax.named_scope("gram"):
        gram, back = call(functools.partial(gram_kernel, n_row), [gram_shape, back_f32], (*parts, first, scale))
        *early, last = direct_rounds(n_col)
        for masks in early:
            gram = call(merge_kernel, gram_shape, [gram] + [partner(gram, "col", mask) for mask in masks])
        grams = [gram] + [partner(gram, "col", mask) for mask in last]
        basis, factor = call(
            functools.partial(factor_kernel, total_cols), [back_f32, shape(width, width)], (*grams, back)
        )
    return basis, factor


def solution(mesh):
    in_specs = (P("row", "col"), P(None, "col"), P("col"), P("row"), P("row"), P("row"))
    out_specs = (P(None, "col"), P())
    return jax.shard_map(local, mesh=mesh, in_specs=in_specs, out_specs=out_specs, check_vma=False)
```

```python
import functools

import jax
import jax.numpy as jnp
from jax import lax
from jax.experimental import pallas as pl
from jax.experimental.pallas import tpu as pltpu
from jax.sharding import PartitionSpec as P

LANES = 128
SUBLANES = 8
HIGHEST = lax.Precision.HIGHEST
F32 = jnp.float32
BF16 = jnp.bfloat16
NT = (((1,), (1,)), ((), ()))
CONE_SPAN = 4
SHIFTS = tuple(range(1 - CONE_SPAN, CONE_SPAN))

VMEM_LIMIT = 16 * 1024 * 1024
VMEM = pl.BlockSpec(memory_space=pltpu.VMEM)
SMEM = pl.BlockSpec(memory_space=pltpu.SMEM)


def call(body, outs, args, scalars=0, flops=0):
    return pl.pallas_call(
        body,
        out_shape=outs,
        in_specs=[SMEM] * scalars + [VMEM] * (len(args) - scalars),
        out_specs=jax.tree.map(lambda _: VMEM, outs),
        cost_estimate=pl.CostEstimate(flops=flops, bytes_accessed=flops // 96, transcendentals=0) if flops else None,
        compiler_params=pltpu.CompilerParams(vmem_limit_bytes=VMEM_LIMIT),
    )(*args)


def partner(value, axis, mask, odd_mask=None):
    odd_mask = mask if odd_mask is None else odd_mask
    size = lax.axis_size(axis)
    return lax.ppermute(value, axis, [(i, i ^ (odd_mask if i % 2 else mask)) for i in range(size)])


def tree_sum(terms):
    while len(terms) > 1:
        terms = [terms[i] + terms[i + 1] for i in range(0, len(terms), 2)]
    return terms[0]


def half_start(rows, core, kept):
    half = rows // 2
    return pl.multiple_of((core if kept else 1 - core) * half, half)


def half_rows(a_ref, core_ref, kept):
    rows = a_ref.shape[0]
    return a_ref[pl.ds(half_start(rows, core_ref[0], kept), rows // 2), :]


def project(scaled, a_half):
    return lax.dot_general(scaled, a_half, NT, preferred_element_type=F32)


def first_send_kernel(core_ref, scaled_ref, a_ref, send_ref):
    send_ref[...] = project(scaled_ref[...], half_rows(a_ref, core_ref, False)).astype(BF16)


def next_send_kernel(terms, core_ref, *refs):
    parts, (scale_ref, a_ref, send_ref, scaled_ref, back_ref) = refs[:terms], refs[terms:]
    scale = scale_ref[...]
    back = tree_sum([part[...].astype(F32) for part in parts]) * scale
    back_ref[...] = back
    scaled = (back * scale).astype(BF16)
    scaled_ref[...] = scaled
    send_ref[...] = project(scaled, half_rows(a_ref, core_ref, False)).astype(BF16)


def keep_kernel(core_ref, scaled_ref, a_ref, keep_ref):
    keep_ref[...] = project(scaled_ref[...], half_rows(a_ref, core_ref, True))


def add_kernel(own_ref, *refs):
    parts, (keep_ref, send_ref) = refs[:-2], refs[-2:]
    total = tree_sum([own_ref[...]] + [part[...].astype(F32) for part in parts])
    keep_ref[...] = total
    send_ref[...] = total.astype(BF16)


def shifted(value, shift):
    if shift == 0:
        return value
    return pltpu.roll(value, (-shift) % value.shape[-1], value.ndim - 1)


def fold_kernel(base_ref, point_ref, id_ref, kind_ref, a_ref, out_ref):
    shape = point_ref.shape
    point, ids = point_ref[...], id_ref[...]
    soc = kind_ref[...] == 1
    place = lax.broadcasted_iota(jnp.int32, shape, 0) * LANES + lax.broadcasted_iota(jnp.int32, shape, 1)
    head = jnp.where(ids == base_ref[0] + place, 1.0, 0.0)
    same = {s: jnp.where(shifted(ids, s) == ids, 1.0, 0.0) for s in SHIFTS}
    tail = jnp.where(soc, point * (1.0 - head), 0.0)
    square = sum(same[s] * shifted(tail * tail, s) for s in SHIFTS)
    norm = jnp.sqrt(jnp.where(soc, square, 1.0))
    ratio = sum(same[s] * shifted(head * point, s) for s in SHIFTS) / norm
    unit = tail / norm
    plain = jnp.where(point > 0, 1.0, 0.0)
    weights = {}
    for s in SHIFTS:
        eye = 1.0 if s == 0 else 0.0
        other = shifted(unit, s)
        at_head = 0.5 * (eye + other)
        at_tail = 0.5 * (unit * shifted(head, s) + (1.0 + ratio) * eye - ratio * unit * other)
        cone = head * at_head + (1.0 - head) * at_tail
        weights[s] = same[s] * jnp.where(soc, cone, plain * eye)
    offset = lax.broadcasted_iota(jnp.int32, (LANES, LANES), 0) - lax.broadcasted_iota(jnp.int32, (LANES, LANES), 1)
    for block in range(shape[0]):
        operator = jnp.zeros((LANES, LANES), F32)
        for s in SHIFTS:
            operator = jnp.where(offset == s, weights[s][block : block + 1, :], operator)
        rows = slice(block * LANES, (block + 1) * LANES)
        folded = jnp.dot(operator, a_ref[rows, :].astype(F32), precision=HIGHEST, preferred_element_type=F32)
        out_ref[rows, :] = folded.astype(BF16)


def round_kernel(keep_ref, got_ref, out_ref):
    out_ref[...] = (keep_ref[...] + got_ref[...].astype(F32)).astype(BF16)


def back_kept_kernel(core_ref, held_ref, a_ref, out_ref):
    out_ref[...] = jnp.dot(held_ref[...], half_rows(a_ref, core_ref, True), preferred_element_type=F32)


def back_kernel(core_ref, kept_ref, got_ref, a_ref, out_ref):
    sent = jnp.dot(got_ref[...], half_rows(a_ref, core_ref, False), preferred_element_type=F32)
    out_ref[...] = (kept_ref[...] + sent).astype(BF16)


def packed_places(width):
    row = lax.broadcasted_iota(jnp.int32, (width, LANES), 0)
    lane = lax.broadcasted_iota(jnp.int32, (width, LANES), 1)
    return lane <= row, lane <= width


def gram_of(value):
    width, cols = value.shape
    padded = jnp.concatenate([value, jnp.zeros((LANES - width, cols), F32)], axis=0)
    return lax.dot_general(value, padded, NT, precision=HIGHEST, preferred_element_type=F32)


def first_gram_kernel(back_ref, gram_ref):
    gram_ref[...] = pltpu.roll(gram_of(back_ref[...]), 1, 1)


def gram_kernel(terms, *refs):
    parts, (first_ref, scale_ref, gram_ref, back_ref) = refs[:terms], refs[terms:]
    back = tree_sum([part[...].astype(F32) for part in parts]) * scale_ref[...]
    back_ref[...] = back
    unit = 1.0 / jnp.maximum(jnp.max(jnp.abs(back), keepdims=True), 1e-37)
    in_second, in_first = packed_places(back.shape[0])
    gram_ref[...] = jnp.where(in_second, gram_of(back * unit), jnp.where(in_first, first_ref[...], unit))


def merge_grams(grams):
    width = grams[0].shape[0]
    units = [gram[:1, LANES - 1 :] for gram in grams]
    unit = functools.reduce(jnp.minimum, units)
    in_second, in_first = packed_places(width)
    grams = [gram[...] for gram in grams]
    second = tree_sum([gram * ((unit / own) * (unit / own)) for gram, own in zip(grams, units)])
    return jnp.where(in_second, second, jnp.where(in_first, tree_sum(grams), unit)), unit


def merge_kernel(*refs):
    *grams, out_ref = refs
    out_ref[...] = merge_grams(grams)[0]


def unpack_grams(packed):
    width = packed.shape[0]
    row = lax.broadcasted_iota(jnp.int32, (width, width), 0)
    lane = lax.broadcasted_iota(jnp.int32, (width, width), 1)
    lower = packed[:, :width]
    upper = pltpu.roll(packed, LANES - 1, 1)[:, :width]
    return jnp.where(lane <= row, lower, lower.T), jnp.where(lane >= row, upper, upper.T)


def splat(value, width):
    return jnp.broadcast_to(value, (SUBLANES, width))


def eliminate_tile(upper, inverse, tile):
    size = upper[0].shape[1]
    first = tile * SUBLANES
    below = range(tile + 1, len(upper))
    steps = range(SUBLANES)
    rows = [splat(upper[tile][t : t + 1, :], size) for t in steps]
    others = [splat(inverse[tile][t : t + 1, :], size) for t in steps]
    corner = {(t, u): splat(rows[t][:, first + u : first + u + 1], size) for t in steps for u in range(t, SUBLANES)}
    columns = [{i: splat(upper[i][:, first + t : first + t + 1], size) for i in below} for t in steps]
    inverted = []
    for t in steps:
        inverted.append(1.0 / corner[t, t])
        for u in range(t + 1, SUBLANES):
            factor = corner[t, u] * inverted[t]
            for w in range(u, SUBLANES):
                corner[u, w] = corner[u, w] - factor * corner[t, w]
            rows[u] = rows[u] - factor * rows[t]
            others[u] = others[u] - factor * others[t]
            for i in below:
                columns[u][i] = columns[u][i] - factor * columns[t][i]
    for i in below:
        factors = [columns[t][i] * inverted[t] for t in steps]
        upper[i] = upper[i] - sum(f * row for f, row in zip(factors, rows))
        inverse[i] = inverse[i] - sum(f * row for f, row in zip(factors, others))
    sub = lax.broadcasted_iota(jnp.int32, (SUBLANES, size), 0)
    pivots, upper[tile], inverse[tile] = corner[0, 0], rows[0], others[0]
    for t in steps[1:]:
        pivots = jnp.where(sub == t, corner[t, t], pivots)
        upper[tile] = jnp.where(sub == t, rows[t], upper[tile])
        inverse[tile] = jnp.where(sub == t, others[t], inverse[tile])
    root = 1.0 / jnp.sqrt(pivots)
    upper[tile], inverse[tile] = upper[tile] * root, inverse[tile] * root


def eliminate(grams):
    size = grams[0].shape[0]
    tiles = range(size // SUBLANES)
    sub = lax.broadcasted_iota(jnp.int32, (SUBLANES, size), 0)
    lane = lax.broadcasted_iota(jnp.int32, (SUBLANES, size), 1)
    uppers = [[gram[i * SUBLANES : (i + 1) * SUBLANES, :] for i in tiles] for gram in grams]
    inverses = [[jnp.where(sub + i * SUBLANES == lane, 1.0, 0.0) for i in tiles] for _ in grams]
    for tile in tiles:
        for upper, inverse in zip(uppers, inverses):
            eliminate_tile(upper, inverse, tile)
    return [(jnp.concatenate(upper, axis=0), jnp.concatenate(inverse, axis=0)) for upper, inverse in zip(uppers, inverses)]


def factor_kernel(total_cols, *refs):
    *grams, back_ref, basis_ref, factor_ref = refs
    width = back_ref.shape[0]
    packed, unit = merge_grams(grams)
    (upper, inverse), (_, inverse_one) = eliminate([gram * (1.0 / total_cols) for gram in unpack_grams(packed)])
    basis_ref[...] = jnp.dot(inverse, back_ref[...] * unit, precision=HIGHEST, preferred_element_type=F32)
    row = lax.broadcasted_iota(jnp.int32, (width, width), 0)
    col = lax.broadcasted_iota(jnp.int32, (width, width), 1)
    upper = jnp.where(row <= col, upper, 0.0)
    factor = lax.dot_general(upper, inverse_one, NT, precision=HIGHEST, preferred_element_type=F32)
    factor_ref[...] = factor / unit


def chip_rounds(size):
    rounds, mask = [], 2
    while mask < size:
        if 2 * mask < size:
            rounds += [(2 * mask, mask), (mask, 2 * mask)]
        else:
            rounds.append((mask, mask))
        mask *= 4
    return rounds


def direct_rounds(size):
    rounds, mask = [[1]], 2
    while mask < size:
        rounds.append([mask, 2 * mask, 3 * mask] if 2 * mask < size else [mask])
        mask *= 4
    return rounds


def local(a_matrix, omega, col_scale, cone_point, cone_id, cone_kind):
    width = omega.shape[0]
    rows, cols = a_matrix.shape
    n_col = lax.axis_size("col")
    n_row = lax.axis_size("row")
    here = lax.axis_index("col")
    total_cols = cols * n_col
    core = lax.rem(here, 2).reshape(1)
    scale = col_scale.reshape(1, cols)
    rounds = chip_rounds(n_col)

    def shape(*dims, dtype=F32):
        return jax.ShapeDtypeStruct(dims, dtype)

    half_f32, half_bf16 = shape(width, rows // 2), shape(width, rows // 2, dtype=BF16)
    back_f32, back_bf16 = shape(width, cols), shape(width, cols, dtype=BF16)

    flops = width * rows * cols

    def fold(after):
        point, after = lax.optimization_barrier((cone_point, after))
        base = (lax.axis_index("row") * rows).reshape(1)
        vectors = [v.reshape(rows // LANES, LANES) for v in (point, cone_id, cone_kind)]
        out = shape(rows, cols, dtype=BF16)
        return call(fold_kernel, out, (base, *vectors, a_matrix), scalars=1, flops=10 * flops), after

    def exchange(keep, send, folded=None):
        got = partner(send, "col", 1)
        for masks in rounds:
            keep, send = call(add_kernel, [half_f32, half_bf16], (keep, got))
            fresh = folded is None
            if fresh:
                folded, send = fold(send)
            got = partner(send, "col", *masks)
            if fresh:
                folded, got = lax.optimization_barrier((folded, got))
        summed = call(round_kernel, half_bf16, (keep, got))
        kept = call(back_kept_kernel, back_f32, (core, summed, folded), scalars=1, flops=flops)
        got = partner(summed, "col", 1)
        part = call(back_kernel, back_bf16, (core, kept, got, folded), scalars=1, flops=flops)
        return folded, [part] + [partner(part, "row", mask) for mask in range(1, n_row)]

    with jax.named_scope("pass_one"):
        scaled = (omega.astype(F32) * scale).astype(BF16)
        send = call(first_send_kernel, half_bf16, (core, scaled, a_matrix), scalars=1)
        keep = call(keep_kernel, half_f32, (core, scaled, a_matrix), scalars=1, flops=flops)
        folded, parts = exchange(keep, send)
    with jax.named_scope("pass_two"):
        send, scaled, back_one = call(
            functools.partial(next_send_kernel, n_row),
            [half_bf16, back_bf16, back_f32],
            (core, *parts, scale, a_matrix),
            scalars=1,
        )
        keep = call(keep_kernel, half_f32, (core, scaled, a_matrix), scalars=1, flops=flops)
        gram_shape = shape(width, LANES)
        first = call(first_gram_kernel, gram_shape, (back_one,), flops=flops // 4)
        _, parts = exchange(keep, send, folded)

    with jax.named_scope("gram"):
        gram, back = call(functools.partial(gram_kernel, n_row), [gram_shape, back_f32], (*parts, first, scale))
        *early, last = direct_rounds(n_col)
        for masks in early:
            gram = call(merge_kernel, gram_shape, [gram] + [partner(gram, "col", mask) for mask in masks])
        grams = [gram] + [partner(gram, "col", mask) for mask in last]
        basis, factor = call(
            functools.partial(factor_kernel, total_cols), [back_f32, shape(width, width)], (*grams, back)
        )
    return basis, factor


def solution(mesh):
    in_specs = (P("row", "col"), P(None, "col"), P("col"), P("row"), P("row"), P("row"))
    out_specs = (P(None, "col"), P())
    return jax.shard_map(local, mesh=mesh, in_specs=in_specs, out_specs=out_specs, check_vma=False)
```

```python
import functools

import jax
import jax.numpy as jnp
from jax import lax
from jax.experimental import pallas as pl
from jax.experimental.pallas import tpu as pltpu
from jax.sharding import PartitionSpec as P

LANES = 128
SUBLANES = 8
HIGHEST = lax.Precision.HIGHEST
F32 = jnp.float32
BF16 = jnp.bfloat16
NT = (((1,), (1,)), ((), ()))
CONE_SPAN = 4
SHIFTS = tuple(range(1 - CONE_SPAN, CONE_SPAN))

VMEM_LIMIT = 16 * 1024 * 1024
FIRST_VMEM_LIMIT = 60 * 1024 * 1024
HBM = pl.BlockSpec(memory_space=pltpu.HBM)
VMEM = pl.BlockSpec(memory_space=pltpu.VMEM)
SMEM = pl.BlockSpec(memory_space=pltpu.SMEM)


def call(body, outs, args, scalars=0, flops=0):
    return pl.pallas_call(
        body,
        out_shape=outs,
        in_specs=[SMEM] * scalars + [VMEM] * (len(args) - scalars),
        out_specs=jax.tree.map(lambda _: VMEM, outs),
        cost_estimate=pl.CostEstimate(flops=flops, bytes_accessed=flops // 96, transcendentals=0) if flops else None,
        compiler_params=pltpu.CompilerParams(vmem_limit_bytes=VMEM_LIMIT),
    )(*args)


def partner(value, axis, mask, odd_mask=None):
    odd_mask = mask if odd_mask is None else odd_mask
    size = lax.axis_size(axis)
    return lax.ppermute(value, axis, [(i, i ^ (odd_mask if i % 2 else mask)) for i in range(size)])


def tree_sum(terms):
    while len(terms) > 1:
        terms = [terms[i] + terms[i + 1] for i in range(0, len(terms), 2)]
    return terms[0]


def half_start(rows, core, kept):
    half = rows // 2
    return pl.multiple_of((core if kept else 1 - core) * half, half)


def half_rows(a_ref, core_ref, kept):
    rows = a_ref.shape[0]
    return a_ref[pl.ds(half_start(rows, core_ref[0], kept), rows // 2), :]


def project(scaled, a_half):
    return lax.dot_general(scaled, a_half, NT, preferred_element_type=F32)


def first_rows_kernel(
    core_ref, omega_hbm, scale_hbm, a_hbm, send_hbm, keep_hbm, omega_ref, scale_ref, a_ref, send_ref, keep_ref, sems
):
    rows = a_hbm.shape[0]

    def copy(source, target, number):
        started = pltpu.make_async_copy(source, target, sems.at[number])
        started.start()
        return started

    into_scale = copy(scale_hbm, scale_ref, 0)
    into_omega = copy(omega_hbm, omega_ref, 1)
    parts = [a_hbm.at[pl.ds(half_start(rows, core_ref[0], kept), rows // 2), :] for kept in (False, True)]
    into_sent, into_kept = [copy(part, a_ref.at[number], 2 + number) for number, part in enumerate(parts)]
    into_scale.wait()
    into_omega.wait()
    scaled = (omega_ref[...].astype(F32) * scale_ref[...]).astype(BF16)
    into_sent.wait()
    send_ref[...] = project(scaled, a_ref[0]).astype(BF16)
    out_send = copy(send_ref, send_hbm, 4)
    into_kept.wait()
    keep_ref[...] = project(scaled, a_ref[1])
    out_keep = copy(keep_ref, keep_hbm, 5)
    out_send.wait()
    out_keep.wait()


def hold_kernel(value_ref, out_ref):
    out_ref[...] = value_ref[...]


def next_send_kernel(terms, core_ref, *refs):
    parts, (scale_ref, a_ref, send_ref, scaled_ref, back_ref) = refs[:terms], refs[terms:]
    scale = scale_ref[...]
    back = tree_sum([part[...].astype(F32) for part in parts]) * scale
    back_ref[...] = back
    scaled = (back * scale).astype(BF16)
    scaled_ref[...] = scaled
    send_ref[...] = project(scaled, half_rows(a_ref, core_ref, False)).astype(BF16)


def keep_kernel(core_ref, scaled_ref, a_ref, keep_ref):
    keep_ref[...] = project(scaled_ref[...], half_rows(a_ref, core_ref, True))


def add_kernel(own_ref, *refs):
    parts, (keep_ref, send_ref) = refs[:-2], refs[-2:]
    total = tree_sum([own_ref[...]] + [part[...].astype(F32) for part in parts])
    keep_ref[...] = total
    send_ref[...] = total.astype(BF16)


def shifted(value, shift):
    if shift == 0:
        return value
    return pltpu.roll(value, (-shift) % value.shape[-1], value.ndim - 1)


def fold_kernel(base_ref, point_ref, id_ref, kind_ref, a_ref, out_ref):
    shape = point_ref.shape
    point, ids = point_ref[...], id_ref[...]
    soc = kind_ref[...] == 1
    place = lax.broadcasted_iota(jnp.int32, shape, 0) * LANES + lax.broadcasted_iota(jnp.int32, shape, 1)
    head = jnp.where(ids == base_ref[0] + place, 1.0, 0.0)
    same = {s: jnp.where(shifted(ids, s) == ids, 1.0, 0.0) for s in SHIFTS}
    tail = jnp.where(soc, point * (1.0 - head), 0.0)
    square = sum(same[s] * shifted(tail * tail, s) for s in SHIFTS)
    norm = jnp.sqrt(jnp.where(soc, square, 1.0))
    ratio = sum(same[s] * shifted(head * point, s) for s in SHIFTS) / norm
    unit = tail / norm
    plain = jnp.where(point > 0, 1.0, 0.0)
    weights = {}
    for s in SHIFTS:
        eye = 1.0 if s == 0 else 0.0
        other = shifted(unit, s)
        at_head = 0.5 * (eye + other)
        at_tail = 0.5 * (unit * shifted(head, s) + (1.0 + ratio) * eye - ratio * unit * other)
        cone = head * at_head + (1.0 - head) * at_tail
        weights[s] = same[s] * jnp.where(soc, cone, plain * eye)
    offset = lax.broadcasted_iota(jnp.int32, (LANES, LANES), 0) - lax.broadcasted_iota(jnp.int32, (LANES, LANES), 1)
    for block in range(shape[0]):
        operator = jnp.zeros((LANES, LANES), F32)
        for s in SHIFTS:
            operator = jnp.where(offset == s, weights[s][block : block + 1, :], operator)
        rows = slice(block * LANES, (block + 1) * LANES)
        folded = jnp.dot(operator, a_ref[rows, :].astype(F32), precision=HIGHEST, preferred_element_type=F32)
        out_ref[rows, :] = folded.astype(BF16)


def round_kernel(keep_ref, got_ref, out_ref):
    out_ref[...] = (keep_ref[...] + got_ref[...].astype(F32)).astype(BF16)


def back_kept_kernel(core_ref, held_ref, a_ref, out_ref):
    out_ref[...] = jnp.dot(held_ref[...], half_rows(a_ref, core_ref, True), preferred_element_type=F32)


def back_kernel(core_ref, kept_ref, got_ref, a_ref, out_ref):
    sent = jnp.dot(got_ref[...], half_rows(a_ref, core_ref, False), preferred_element_type=F32)
    out_ref[...] = (kept_ref[...] + sent).astype(BF16)


def packed_places(width):
    row = lax.broadcasted_iota(jnp.int32, (width, LANES), 0)
    lane = lax.broadcasted_iota(jnp.int32, (width, LANES), 1)
    return lane <= row, lane <= width


def gram_of(value):
    width, cols = value.shape
    padded = jnp.concatenate([value, jnp.zeros((LANES - width, cols), F32)], axis=0)
    return lax.dot_general(value, padded, NT, precision=HIGHEST, preferred_element_type=F32)


def first_gram_kernel(back_ref, gram_ref):
    gram_ref[...] = pltpu.roll(gram_of(back_ref[...]), 1, 1)


def gram_kernel(terms, *refs):
    parts, (first_ref, scale_ref, gram_ref, back_ref) = refs[:terms], refs[terms:]
    back = tree_sum([part[...].astype(F32) for part in parts]) * scale_ref[...]
    back_ref[...] = back
    unit = 1.0 / jnp.maximum(jnp.max(jnp.abs(back), keepdims=True), 1e-37)
    in_second, in_first = packed_places(back.shape[0])
    gram_ref[...] = jnp.where(in_second, gram_of(back * unit), jnp.where(in_first, first_ref[...], unit))


def merge_grams(grams):
    width = grams[0].shape[0]
    units = [gram[:1, LANES - 1 :] for gram in grams]
    unit = functools.reduce(jnp.minimum, units)
    in_second, in_first = packed_places(width)
    grams = [gram[...] for gram in grams]
    second = tree_sum([gram * ((unit / own) * (unit / own)) for gram, own in zip(grams, units)])
    return jnp.where(in_second, second, jnp.where(in_first, tree_sum(grams), unit)), unit


def merge_kernel(*refs):
    *grams, out_ref = refs
    out_ref[...] = merge_grams(grams)[0]


def unpack_grams(packed):
    width = packed.shape[0]
    row = lax.broadcasted_iota(jnp.int32, (width, width), 0)
    lane = lax.broadcasted_iota(jnp.int32, (width, width), 1)
    lower = packed[:, :width]
    upper = pltpu.roll(packed, LANES - 1, 1)[:, :width]
    return jnp.where(lane <= row, lower, lower.T), jnp.where(lane >= row, upper, upper.T)


def splat(value, width):
    return jnp.broadcast_to(value, (SUBLANES, width))


def eliminate_tile(upper, inverse, tile):
    size = upper[0].shape[1]
    first = tile * SUBLANES
    below = range(tile + 1, len(upper))
    steps = range(SUBLANES)
    rows = [splat(upper[tile][t : t + 1, :], size) for t in steps]
    others = [splat(inverse[tile][t : t + 1, :], size) for t in steps]
    corner = {(t, u): splat(rows[t][:, first + u : first + u + 1], size) for t in steps for u in range(t, SUBLANES)}
    columns = [{i: splat(upper[i][:, first + t : first + t + 1], size) for i in below} for t in steps]
    inverted = []
    for t in steps:
        inverted.append(1.0 / corner[t, t])
        for u in range(t + 1, SUBLANES):
            factor = corner[t, u] * inverted[t]
            for w in range(u, SUBLANES):
                corner[u, w] = corner[u, w] - factor * corner[t, w]
            rows[u] = rows[u] - factor * rows[t]
            others[u] = others[u] - factor * others[t]
            for i in below:
                columns[u][i] = columns[u][i] - factor * columns[t][i]
    for i in below:
        factors = [columns[t][i] * inverted[t] for t in steps]
        upper[i] = upper[i] - sum(f * row for f, row in zip(factors, rows))
        inverse[i] = inverse[i] - sum(f * row for f, row in zip(factors, others))
    sub = lax.broadcasted_iota(jnp.int32, (SUBLANES, size), 0)
    pivots, upper[tile], inverse[tile] = corner[0, 0], rows[0], others[0]
    for t in steps[1:]:
        pivots = jnp.where(sub == t, corner[t, t], pivots)
        upper[tile] = jnp.where(sub == t, rows[t], upper[tile])
        inverse[tile] = jnp.where(sub == t, others[t], inverse[tile])
    root = 1.0 / jnp.sqrt(pivots)
    upper[tile], inverse[tile] = upper[tile] * root, inverse[tile] * root


def eliminate(grams):
    size = grams[0].shape[0]
    tiles = range(size // SUBLANES)
    sub = lax.broadcasted_iota(jnp.int32, (SUBLANES, size), 0)
    lane = lax.broadcasted_iota(jnp.int32, (SUBLANES, size), 1)
    uppers = [[gram[i * SUBLANES : (i + 1) * SUBLANES, :] for i in tiles] for gram in grams]
    inverses = [[jnp.where(sub + i * SUBLANES == lane, 1.0, 0.0) for i in tiles] for _ in grams]
    for tile in tiles:
        for upper, inverse in zip(uppers, inverses):
            eliminate_tile(upper, inverse, tile)
    return [(jnp.concatenate(upper, axis=0), jnp.concatenate(inverse, axis=0)) for upper, inverse in zip(uppers, inverses)]


def factor_kernel(total_cols, *refs):
    *grams, back_ref, basis_ref, factor_ref = refs
    width = back_ref.shape[0]
    packed, unit = merge_grams(grams)
    (upper, inverse), (_, inverse_one) = eliminate([gram * (1.0 / total_cols) for gram in unpack_grams(packed)])
    basis_ref[...] = jnp.dot(inverse, back_ref[...] * unit, precision=HIGHEST, preferred_element_type=F32)
    row = lax.broadcasted_iota(jnp.int32, (width, width), 0)
    col = lax.broadcasted_iota(jnp.int32, (width, width), 1)
    upper = jnp.where(row <= col, upper, 0.0)
    factor = lax.dot_general(upper, inverse_one, NT, precision=HIGHEST, preferred_element_type=F32)
    factor_ref[...] = factor / unit


def chip_rounds(size):
    rounds, mask = [], 2
    while mask < size:
        if 2 * mask < size:
            rounds += [(2 * mask, mask), (mask, 2 * mask)]
        else:
            rounds.append((mask, mask))
        mask *= 4
    return rounds


def direct_rounds(size):
    rounds, mask = [[1]], 2
    while mask < size:
        rounds.append([mask, 2 * mask, 3 * mask] if 2 * mask < size else [mask])
        mask *= 4
    return rounds


def local(a_matrix, omega, col_scale, cone_point, cone_id, cone_kind):
    width = omega.shape[0]
    rows, cols = a_matrix.shape
    n_col = lax.axis_size("col")
    n_row = lax.axis_size("row")
    here = lax.axis_index("col")
    total_cols = cols * n_col
    core = lax.rem(here, 2).reshape(1)
    scale = col_scale.reshape(1, cols)
    rounds = chip_rounds(n_col)

    def shape(*dims, dtype=F32):
        return jax.ShapeDtypeStruct(dims, dtype)

    half_f32, half_bf16 = shape(width, rows // 2), shape(width, rows // 2, dtype=BF16)
    back_f32, back_bf16 = shape(width, cols), shape(width, cols, dtype=BF16)

    flops = width * rows * cols

    def fold(after):
        point, after = lax.optimization_barrier((cone_point, after))
        base = (lax.axis_index("row") * rows).reshape(1)
        vectors = [v.reshape(rows // LANES, LANES) for v in (point, cone_id, cone_kind)]
        out = shape(rows, cols, dtype=BF16)
        return call(fold_kernel, out, (base, *vectors, a_matrix), scalars=1, flops=10 * flops), after

    def exchange(keep, send, folded=None):
        got = partner(send, "col", 1)
        for masks in rounds:
            keep, send = call(add_kernel, [half_f32, half_bf16], (keep, got))
            fresh = folded is None
            if fresh:
                folded, send = fold(send)
            got = partner(send, "col", *masks)
            if fresh:
                folded, got = lax.optimization_barrier((folded, got))
        summed = call(round_kernel, half_bf16, (keep, got))
        kept = call(back_kept_kernel, back_f32, (core, summed, folded), scalars=1, flops=flops)
        got = partner(summed, "col", 1)
        part = call(back_kernel, back_bf16, (core, kept, got, folded), scalars=1, flops=flops)
        return folded, [part] + [partner(part, "row", mask) for mask in range(1, n_row)]

    with jax.named_scope("pass_one"):
        send, keep = pl.pallas_call(
            first_rows_kernel,
            out_shape=[half_bf16, half_f32],
            in_specs=[SMEM, HBM, HBM, HBM],
            out_specs=[HBM, HBM],
            scratch_shapes=[
                pltpu.VMEM(omega.shape, BF16),
                pltpu.VMEM(scale.shape, F32),
                pltpu.VMEM((2, rows // 2, cols), BF16),
                pltpu.VMEM(half_bf16.shape, BF16),
                pltpu.VMEM(half_f32.shape, F32),
                pltpu.SemaphoreType.DMA((6,)),
            ],
            compiler_params=pltpu.CompilerParams(vmem_limit_bytes=FIRST_VMEM_LIMIT),
        )(core, omega, scale, a_matrix)
        keep = call(hold_kernel, half_f32, (keep,), flops=flops)
        folded, parts = exchange(keep, send)
    with jax.named_scope("pass_two"):
        send, scaled, back_one = call(
            functools.partial(next_send_kernel, n_row),
            [half_bf16, back_bf16, back_f32],
            (core, *parts, scale, a_matrix),
            scalars=1,
        )
        keep = call(keep_kernel, half_f32, (core, scaled, a_matrix), scalars=1, flops=flops)
        gram_shape = shape(width, LANES)
        first = call(first_gram_kernel, gram_shape, (back_one,), flops=flops // 4)
        _, parts = exchange(keep, send, folded)

    with jax.named_scope("gram"):
        gram, back = call(functools.partial(gram_kernel, n_row), [gram_shape, back_f32], (*parts, first, scale))
        *early, last = direct_rounds(n_col)
        for masks in early:
            gram = call(merge_kernel, gram_shape, [gram] + [partner(gram, "col", mask) for mask in masks])
        grams = [gram] + [partner(gram, "col", mask) for mask in last]
        basis, factor = call(
            functools.partial(factor_kernel, total_cols), [back_f32, shape(width, width)], (*grams, back)
        )
    return basis, factor


def solution(mesh):
    in_specs = (P("row", "col"), P(None, "col"), P("col"), P("row"), P("row"), P("row"))
    out_specs = (P(None, "col"), P())
    return jax.shard_map(local, mesh=mesh, in_specs=in_specs, out_specs=out_specs, check_vma=False)
```

```python
import functools

import jax
import jax.numpy as jnp
from jax import lax
from jax.experimental import pallas as pl
from jax.experimental.pallas import tpu as pltpu
from jax.sharding import PartitionSpec as P

LANES = 128
SUBLANES = 8
HIGHEST = lax.Precision.HIGHEST
F32 = jnp.float32
BF16 = jnp.bfloat16
NT = (((1,), (1,)), ((), ()))
CONE_SPAN = 4
SHIFTS = tuple(range(1 - CONE_SPAN, CONE_SPAN))

VMEM_LIMIT = 16 * 1024 * 1024
FIRST_VMEM_LIMIT = 60 * 1024 * 1024
HBM = pl.BlockSpec(memory_space=pltpu.HBM)
VMEM = pl.BlockSpec(memory_space=pltpu.VMEM)
SMEM = pl.BlockSpec(memory_space=pltpu.SMEM)


def call(body, outs, args, scalars=0, flops=0):
    return pl.pallas_call(
        body,
        out_shape=outs,
        in_specs=[SMEM] * scalars + [VMEM] * (len(args) - scalars),
        out_specs=jax.tree.map(lambda _: VMEM, outs),
        cost_estimate=pl.CostEstimate(flops=flops, bytes_accessed=flops // 96, transcendentals=0) if flops else None,
        compiler_params=pltpu.CompilerParams(vmem_limit_bytes=VMEM_LIMIT),
    )(*args)


def partner(value, axis, mask, odd_mask=None):
    odd_mask = mask if odd_mask is None else odd_mask
    size = lax.axis_size(axis)
    return lax.ppermute(value, axis, [(i, i ^ (odd_mask if i % 2 else mask)) for i in range(size)])


def tree_sum(terms):
    while len(terms) > 1:
        terms = [terms[i] + terms[i + 1] for i in range(0, len(terms), 2)]
    return terms[0]


def half_start(rows, core, kept):
    half = rows // 2
    return pl.multiple_of((core if kept else 1 - core) * half, half)


def half_rows(a_ref, core_ref, kept):
    rows = a_ref.shape[0]
    return a_ref[pl.ds(half_start(rows, core_ref[0], kept), rows // 2), :]


def project(scaled, a_half):
    return lax.dot_general(scaled, a_half, NT, preferred_element_type=F32)


def first_rows_kernel(
    core_ref, omega_hbm, scale_hbm, a_hbm, send_hbm, keep_hbm, omega_ref, scale_ref, a_ref, send_ref, keep_ref, sems
):
    rows = a_hbm.shape[0]

    def copy(source, target, number):
        started = pltpu.make_async_copy(source, target, sems.at[number])
        started.start()
        return started

    into_scale = copy(scale_hbm, scale_ref, 0)
    into_omega = copy(omega_hbm, omega_ref, 1)
    parts = [a_hbm.at[pl.ds(half_start(rows, core_ref[0], kept), rows // 2), :] for kept in (False, True)]
    into_sent, into_kept = [copy(part, a_ref.at[number], 2 + number) for number, part in enumerate(parts)]
    into_scale.wait()
    into_omega.wait()
    scaled = (omega_ref[...].astype(F32) * scale_ref[...]).astype(BF16)
    into_sent.wait()
    send_ref[...] = project(scaled, a_ref[0]).astype(BF16)
    out_send = copy(send_ref, send_hbm, 4)
    into_kept.wait()
    keep_ref[...] = project(scaled, a_ref[1])
    out_keep = copy(keep_ref, keep_hbm, 5)
    out_send.wait()
    out_keep.wait()


def hold_kernel(value_ref, out_ref):
    out_ref[...] = value_ref[...]


def next_send_kernel(terms, core_ref, *refs):
    parts, (scale_ref, a_ref, send_ref, scaled_ref, back_ref) = refs[:terms], refs[terms:]
    scale = scale_ref[...]
    back = tree_sum([part[...].astype(F32) for part in parts]) * scale
    back_ref[...] = back
    scaled = (back * scale).astype(BF16)
    scaled_ref[...] = scaled
    send_ref[...] = project(scaled, half_rows(a_ref, core_ref, False)).astype(BF16)


def keep_kernel(core_ref, scaled_ref, a_ref, keep_ref):
    keep_ref[...] = project(scaled_ref[...], half_rows(a_ref, core_ref, True))


def add_kernel(own_ref, *refs):
    parts, (keep_ref, send_ref) = refs[:-2], refs[-2:]
    total = tree_sum([own_ref[...]] + [part[...].astype(F32) for part in parts])
    keep_ref[...] = total
    send_ref[...] = total.astype(BF16)


def shifted(value, shift):
    if shift == 0:
        return value
    return pltpu.roll(value, (-shift) % value.shape[-1], value.ndim - 1)


def fold_kernel(base_ref, point_ref, id_ref, kind_ref, a_ref, out_ref):
    shape = point_ref.shape
    point, ids = point_ref[...], id_ref[...]
    soc = kind_ref[...] == 1
    place = lax.broadcasted_iota(jnp.int32, shape, 0) * LANES + lax.broadcasted_iota(jnp.int32, shape, 1)
    head = jnp.where(ids == base_ref[0] + place, 1.0, 0.0)
    same = {s: jnp.where(shifted(ids, s) == ids, 1.0, 0.0) for s in SHIFTS}
    tail = jnp.where(soc, point * (1.0 - head), 0.0)
    square = sum(same[s] * shifted(tail * tail, s) for s in SHIFTS)
    norm = jnp.sqrt(jnp.where(soc, square, 1.0))
    ratio = sum(same[s] * shifted(head * point, s) for s in SHIFTS) / norm
    unit = tail / norm
    plain = jnp.where(point > 0, 1.0, 0.0)
    weights = {}
    for s in SHIFTS:
        eye = 1.0 if s == 0 else 0.0
        other = shifted(unit, s)
        at_head = 0.5 * (eye + other)
        at_tail = 0.5 * (unit * shifted(head, s) + (1.0 + ratio) * eye - ratio * unit * other)
        cone = head * at_head + (1.0 - head) * at_tail
        weights[s] = same[s] * jnp.where(soc, cone, plain * eye)
    offset = lax.broadcasted_iota(jnp.int32, (LANES, LANES), 0) - lax.broadcasted_iota(jnp.int32, (LANES, LANES), 1)
    for block in range(shape[0]):
        operator = jnp.zeros((LANES, LANES), F32)
        for s in SHIFTS:
            operator = jnp.where(offset == s, weights[s][block : block + 1, :], operator)
        rows = slice(block * LANES, (block + 1) * LANES)
        folded = jnp.dot(operator, a_ref[rows, :].astype(F32), precision=HIGHEST, preferred_element_type=F32)
        out_ref[rows, :] = folded.astype(BF16)


def round_kernel(keep_ref, got_ref, out_ref):
    out_ref[...] = (keep_ref[...] + got_ref[...].astype(F32)).astype(BF16)


def back_kept_kernel(core_ref, held_ref, a_ref, out_ref):
    out_ref[...] = jnp.dot(held_ref[...], half_rows(a_ref, core_ref, True), preferred_element_type=F32)


def back_kernel(core_ref, kept_ref, got_ref, a_ref, out_ref):
    sent = jnp.dot(got_ref[...], half_rows(a_ref, core_ref, False), preferred_element_type=F32)
    out_ref[...] = (kept_ref[...] + sent).astype(BF16)


def gram_of(value):
    width, cols = value.shape
    padded = jnp.concatenate([value, jnp.zeros((LANES - width, cols), F32)], axis=0)
    return lax.dot_general(value, padded, NT, precision=HIGHEST, preferred_element_type=F32)


def first_gram_kernel(back_ref, gram_ref):
    gram_ref[...] = gram_of(back_ref[...])


def sum_kernel(*refs):
    *terms, out_ref = refs
    out_ref[...] = tree_sum([term[...] for term in terms])


def in_gram(width):
    return lax.broadcasted_iota(jnp.int32, (width, LANES), 1) < width


def gram_kernel(terms, *refs):
    parts, (scale_ref, gram_ref, back_ref) = refs[:terms], refs[terms:]
    back = tree_sum([part[...].astype(F32) for part in parts]) * scale_ref[...]
    back_ref[...] = back
    unit = 1.0 / jnp.maximum(jnp.max(jnp.abs(back), keepdims=True), 1e-37)
    gram_ref[...] = jnp.where(in_gram(back.shape[0]), gram_of(back * unit), unit)


def merge_grams(grams):
    units = [gram[:1, LANES - 1 :] for gram in grams]
    unit = functools.reduce(jnp.minimum, units)
    total = tree_sum([gram[...] * ((unit / own) * (unit / own)) for gram, own in zip(grams, units)])
    return jnp.where(in_gram(total.shape[0]), total, unit), unit


def merge_kernel(*refs):
    *grams, out_ref = refs
    out_ref[...] = merge_grams(grams)[0]


def splat(value, width):
    return jnp.broadcast_to(value, (SUBLANES, width))


def eliminate_tile(upper, inverse, tile):
    size = upper[0].shape[1]
    first = tile * SUBLANES
    below = range(tile + 1, len(upper))
    steps = range(SUBLANES)
    rows = [splat(upper[tile][t : t + 1, :], size) for t in steps]
    others = [splat(inverse[tile][t : t + 1, :], size) for t in steps]
    corner = {(t, u): splat(rows[t][:, first + u : first + u + 1], size) for t in steps for u in range(t, SUBLANES)}
    columns = [{i: splat(upper[i][:, first + t : first + t + 1], size) for i in below} for t in steps]
    inverted = []
    for t in steps:
        inverted.append(1.0 / corner[t, t])
        for u in range(t + 1, SUBLANES):
            factor = corner[t, u] * inverted[t]
            for w in range(u, SUBLANES):
                corner[u, w] = corner[u, w] - factor * corner[t, w]
            rows[u] = rows[u] - factor * rows[t]
            others[u] = others[u] - factor * others[t]
            for i in below:
                columns[u][i] = columns[u][i] - factor * columns[t][i]
    for i in below:
        factors = [columns[t][i] * inverted[t] for t in steps]
        upper[i] = upper[i] - sum(f * row for f, row in zip(factors, rows))
        inverse[i] = inverse[i] - sum(f * row for f, row in zip(factors, others))
    sub = lax.broadcasted_iota(jnp.int32, (SUBLANES, size), 0)
    pivots, upper[tile], inverse[tile] = corner[0, 0], rows[0], others[0]
    for t in steps[1:]:
        pivots = jnp.where(sub == t, corner[t, t], pivots)
        upper[tile] = jnp.where(sub == t, rows[t], upper[tile])
        inverse[tile] = jnp.where(sub == t, others[t], inverse[tile])
    root = 1.0 / jnp.sqrt(pivots)
    upper[tile], inverse[tile] = upper[tile] * root, inverse[tile] * root


def eliminate(grams):
    size = grams[0].shape[0]
    tiles = range(size // SUBLANES)
    sub = lax.broadcasted_iota(jnp.int32, (SUBLANES, size), 0)
    lane = lax.broadcasted_iota(jnp.int32, (SUBLANES, size), 1)
    uppers = [[gram[i * SUBLANES : (i + 1) * SUBLANES, :] for i in tiles] for gram in grams]
    inverses = [[jnp.where(sub + i * SUBLANES == lane, 1.0, 0.0) for i in tiles] for _ in grams]
    for tile in tiles:
        for upper, inverse in zip(uppers, inverses):
            eliminate_tile(upper, inverse, tile)
    return [(jnp.concatenate(upper, axis=0), jnp.concatenate(inverse, axis=0)) for upper, inverse in zip(uppers, inverses)]


def invert_kernel(total_cols, *refs):
    *grams, out_ref = refs
    width = out_ref.shape[0]
    total = tree_sum([gram[...] for gram in grams])[:, :width]
    ((_, out_ref[...]),) = eliminate([total * (1.0 / total_cols)])


def factor_kernel(total_cols, *refs):
    *grams, inverse_one_ref, back_ref, basis_ref, factor_ref = refs
    width = back_ref.shape[0]
    total, unit = merge_grams(grams)
    ((upper, inverse),) = eliminate([total[:, :width] * (1.0 / total_cols)])
    basis_ref[...] = jnp.dot(inverse, back_ref[...] * unit, precision=HIGHEST, preferred_element_type=F32)
    row = lax.broadcasted_iota(jnp.int32, (width, width), 0)
    col = lax.broadcasted_iota(jnp.int32, (width, width), 1)
    upper = jnp.where(row <= col, upper, 0.0)
    factor = lax.dot_general(upper, inverse_one_ref[...], NT, precision=HIGHEST, preferred_element_type=F32)
    factor_ref[...] = factor / unit


def chip_rounds(size):
    rounds, mask = [], 2
    while mask < size:
        if 2 * mask < size:
            rounds += [(2 * mask, mask), (mask, 2 * mask)]
        else:
            rounds.append((mask, mask))
        mask *= 4
    return rounds


def direct_rounds(size):
    rounds, mask = [[1]], 2
    while mask < size:
        rounds.append([mask, 2 * mask, 3 * mask] if 2 * mask < size else [mask])
        mask *= 4
    return rounds


def local(a_matrix, omega, col_scale, cone_point, cone_id, cone_kind):
    width = omega.shape[0]
    rows, cols = a_matrix.shape
    n_col = lax.axis_size("col")
    n_row = lax.axis_size("row")
    here = lax.axis_index("col")
    total_cols = cols * n_col
    core = lax.rem(here, 2).reshape(1)
    scale = col_scale.reshape(1, cols)
    rounds = chip_rounds(n_col)

    def shape(*dims, dtype=F32):
        return jax.ShapeDtypeStruct(dims, dtype)

    half_f32, half_bf16 = shape(width, rows // 2), shape(width, rows // 2, dtype=BF16)
    back_f32, back_bf16 = shape(width, cols), shape(width, cols, dtype=BF16)

    flops = width * rows * cols

    def fold(after):
        point, after = lax.optimization_barrier((cone_point, after))
        base = (lax.axis_index("row") * rows).reshape(1)
        vectors = [v.reshape(rows // LANES, LANES) for v in (point, cone_id, cone_kind)]
        out = shape(rows, cols, dtype=BF16)
        return call(fold_kernel, out, (base, *vectors, a_matrix), scalars=1, flops=10 * flops), after

    *early, last = direct_rounds(n_col)
    gram_shape = shape(width, LANES)

    def sends(gram, masks):
        return [gram] + [partner(gram, "col", mask) for mask in masks]

    def exchange(keep, send, folded=None, back_one=None):
        got, grams = partner(send, "col", 1), None
        for number, masks in enumerate(rounds):
            keep, send = call(add_kernel, [half_f32, half_bf16], (keep, got))
            fresh = folded is None
            if fresh:
                folded, send = fold(send)
            if back_one is not None:
                if number == 0:
                    back_one, send = lax.optimization_barrier((back_one, send))
                    gram = call(first_gram_kernel, gram_shape, (back_one,), flops=flops // 4)
                else:
                    grams, _ = lax.optimization_barrier((grams, send))
                    gram = call(sum_kernel, gram_shape, grams)
            got = partner(send, "col", *masks)
            if back_one is not None and number == 0:
                gram, got = lax.optimization_barrier((gram, got))
            if back_one is not None:
                grams = (gram, partner(gram, "col", *masks))
            if fresh:
                folded, got = lax.optimization_barrier((folded, got))
        summed = call(round_kernel, half_bf16, (keep, got))
        kept = call(back_kept_kernel, back_f32, (core, summed, folded), scalars=1, flops=flops)
        got = partner(summed, "col", 1)
        part = call(back_kernel, back_bf16, (core, kept, got, folded), scalars=1, flops=flops)
        if back_one is not None:
            grams, _ = lax.optimization_barrier((grams, part))
            grams = sends(call(sum_kernel, gram_shape, grams), [1])
        return folded, grams, [part] + [partner(part, "row", mask) for mask in range(1, n_row)]

    with jax.named_scope("pass_one"):
        send, keep = pl.pallas_call(
            first_rows_kernel,
            out_shape=[half_bf16, half_f32],
            in_specs=[SMEM, HBM, HBM, HBM],
            out_specs=[HBM, HBM],
            scratch_shapes=[
                pltpu.VMEM(omega.shape, BF16),
                pltpu.VMEM(scale.shape, F32),
                pltpu.VMEM((2, rows // 2, cols), BF16),
                pltpu.VMEM(half_bf16.shape, BF16),
                pltpu.VMEM(half_f32.shape, F32),
                pltpu.SemaphoreType.DMA((6,)),
            ],
            compiler_params=pltpu.CompilerParams(vmem_limit_bytes=FIRST_VMEM_LIMIT),
        )(core, omega, scale, a_matrix)
        keep = call(hold_kernel, half_f32, (keep,), flops=flops)
        folded, _, parts = exchange(keep, send)
    with jax.named_scope("pass_two"):
        send, scaled, back_one = call(
            functools.partial(next_send_kernel, n_row),
            [half_bf16, back_bf16, back_f32],
            (core, *parts, scale, a_matrix),
            scalars=1,
        )
        keep = call(keep_kernel, half_f32, (core, scaled, a_matrix), scalars=1, flops=flops)
        _, first_grams, parts = exchange(keep, send, folded, back_one)

    with jax.named_scope("gram"):
        gram, back = call(functools.partial(gram_kernel, n_row), [gram_shape, back_f32], (*parts, scale))
        for masks in early:
            gram = call(merge_kernel, gram_shape, sends(gram, masks))
        first_grams, gram = lax.optimization_barrier((first_grams, gram))
        grams = sends(gram, last)
        inverse_one = call(
            functools.partial(invert_kernel, total_cols), shape(width, width), first_grams, flops=20 * flops
        )
        basis, factor = call(
            functools.partial(factor_kernel, total_cols),
            [back_f32, shape(width, width)],
            (*grams, inverse_one, back),
        )
    return basis, factor


def solution(mesh):
    in_specs = (P("row", "col"), P(None, "col"), P("col"), P("row"), P("row"), P("row"))
    out_specs = (P(None, "col"), P())
    return jax.shard_map(local, mesh=mesh, in_specs=in_specs, out_specs=out_specs, check_vma=False)
```
